256 devices in a mesh: tm: 16 (over x_lo, z), space: 2 (over core), tensor: 8 (over y, x_hi).
Axes of the slice: x: 4 (x_hi: 2, x_lo: 2; x = x_hi * 2 + x_lo), y: 4, z: 8, core: 2. Of those that a mesh axis runs over, the one named last changes fastest.
Arguments:
- queries: bfloat16 [16, 2, 2, 256, 2048], P('tm', 'space', None, None, 'tensor'), may hold values from -12 to 12
- keys: bfloat16 [16, 2, 2, 256, 2048], P('tm', 'space', None, None, 'tensor'), may hold values from -6 to 6
- values: bfloat16 [16, 2, 2, 256, 2048], P('tm', 'space', None, None, 'tensor'), may hold values from -6 to 6
- attention_output: bfloat16 [16, 2, 2, 256, 2048], P('tm', 'space', None, None, 'tensor'), may hold values from -6 to 6
- row_logsumexp: float32 [16, 2, 2, 16, 256], P('tm', 'space', None, 'tensor'), may hold values from 8 to 10.5
- output_cotangent: bfloat16 [16, 2, 2, 256, 3072], P('tm', 'space'), may hold values from -24 to 24
- output_weight: bfloat16 [2048, 3072], P('tensor'), may hold values from -0.109375 to 0.109375
- adapter_down: bfloat16 [2048, 32], P('tensor'), may hold values from -0.109375 to 0.109375
- adapter_up: bfloat16 [32, 3072], replicated, may hold values from -0.109375 to 0.109375
- head_tile_reach: int32 [16, 3], P('tensor'), may hold values from 0 to 1, as said below
- key_tile_valid: int32 [16, 2, 2], replicated, may hold values from 0 to 1, as said below
Outputs:
- grad_q: bfloat16 [16, 2, 2, 256, 2048], P('tm', 'space', None, None, 'tensor')
- grad_k: bfloat16 [16, 2, 2, 256, 2048], P('tm', 'space', None, None, 'tensor')
- grad_v: bfloat16 [16, 2, 2, 256, 2048], P('tm', 'space', None, None, 'tensor')
- grad_a: float32 [2048, 32], P('tensor')
- up_map_gradient: float32 [32, 3072], P(None, 'tensor')
The draws below stay inside these ranges and needn't reach their ends.
Inputs may be any that keep to these rules, and one draw needn't show every extreme that they name: `head_tile_reach`: columns are the reach along frames, height and width; in every aligned group of 2 heads some head has reach 1 on all three. `key_tile_valid`: A tile is 0 exactly when it lies in the last p frame tiles or, where q is 1, in the last width tile; p is 1 to 4 and q is 0 or 1, drawn for the whole grid.
All inputs are finite; a program needn't handle non-finite values.
Results may differ from the reference program's by a relative error of at most 0.011.
Values may be sent and summed in bfloat16 or wider, within the bound.
A program may use at most 128 MiB of HBM per device.

```python
import jax
import jax.numpy as jnp
from jax import lax

MODEL_DIM = 3072
HD = 128
HEADS_DEV = 2
ADAPTER_RANK = 32
TILE = 256
HEADS = 16
ATTENTION_WIDTH = 2048
TIME_TILES = 16
HEIGHT_TILES = 2
WIDTH_TILES = 2
LATENT_TOKENS = 16384


def draw_head_tile_reach(key, part):
    key = jax.random.fold_in(key, 7)
    first_key, second_key = jax.random.split(key)
    drawn = jax.random.randint(first_key, (HEADS, 3), 0, 2)
    groups = HEADS // HEADS_DEV
    picked = jax.random.randint(second_key, (groups,), 0, HEADS_DEV)
    within = jnp.arange(HEADS) % HEADS_DEV
    chosen = within == jnp.repeat(picked, HEADS_DEV)
    return jnp.where(chosen[:, None], 1, drawn).astype(jnp.int32)


def draw_key_tile_valid(key, part):
    key = jax.random.fold_in(key, 11)
    first_key, second_key = jax.random.split(key)
    pad_time = jax.random.randint(first_key, (), 1, 5)
    pad_width = jax.random.randint(second_key, (), 0, 2)
    time_ids = jnp.arange(TIME_TILES)[:, None, None]
    width_ids = jnp.arange(WIDTH_TILES)[None, None, :]
    valid = (time_ids < TIME_TILES - pad_time) & (width_ids < WIDTH_TILES - pad_width)
    valid = jnp.broadcast_to(valid, (TIME_TILES, HEIGHT_TILES, WIDTH_TILES))
    return valid.astype(jnp.int32)


def shard_levels(stream_key, shape, cuts, low, high):
    def one(dim, blocks):
        heights = jax.random.uniform(jax.random.fold_in(jax.random.fold_in(stream_key, 6), dim), (blocks,), jnp.float32, low / len(cuts), high / len(cuts))
        return jnp.repeat(jnp.exp(heights), shape[dim] // blocks).reshape((-1,) + (1,) * (len(shape) - dim - 1))

    level = one(*cuts[0])
    for cut in cuts[1:]:
        level = level * one(*cut)
    return level


def bell_draw(rng, shape, spread, bound, pieces=(), kind=jnp.bfloat16):
    values = jax.random.normal(rng, shape, jnp.float32) * spread
    if len(pieces) > 0:
        values = shard_levels(rng, shape, pieces, -0.22, 0.18) * values
    return jnp.clip(values, min=-bound, max=bound).astype(kind)


def setup_inputs(seed: int = 0) -> dict:
    streams_of = jax.random.split(jax.random.key(seed), 12)
    queries = bell_draw(streams_of[0], (TIME_TILES, HEIGHT_TILES, WIDTH_TILES, TILE, ATTENTION_WIDTH), 2.0, 12.0, ((0, 16), (1, 2), (4, 8)))
    keys = bell_draw(streams_of[1], (TIME_TILES, HEIGHT_TILES, WIDTH_TILES, TILE, ATTENTION_WIDTH), 1.0, 6.0, ((0, 16), (1, 2), (4, 8)))
    values = bell_draw(streams_of[2], (TIME_TILES, HEIGHT_TILES, WIDTH_TILES, TILE, ATTENTION_WIDTH), 1.0, 6.0, ((0, 16), (1, 2), (4, 8)))
    attention_output = bell_draw(streams_of[3], (TIME_TILES, HEIGHT_TILES, WIDTH_TILES, TILE, ATTENTION_WIDTH), 1.0, 6.0, ((0, 16), (1, 2), (4, 8)))
    row_logsumexp = jnp.clip(8.0 + 2.5 * jax.random.uniform(streams_of[4], (TIME_TILES, HEIGHT_TILES, WIDTH_TILES, HEADS, TILE), jnp.float32) ** shard_levels(streams_of[4], (TIME_TILES, HEIGHT_TILES, WIDTH_TILES, HEADS, TILE), ((0, 16), (1, 2), (3, 8)), -0.2, 0.2), 8.0, 10.5)
    output_cotangent = bell_draw(streams_of[5], (TIME_TILES, HEIGHT_TILES, WIDTH_TILES, TILE, MODEL_DIM), 4.0, 24.0, ((0, 16), (1, 2)))
    output_weight = bell_draw(streams_of[6], (ATTENTION_WIDTH, MODEL_DIM), MODEL_DIM ** -0.5, 0.109375, ((0, 8),))
    adapter_down = bell_draw(streams_of[7], (ATTENTION_WIDTH, ADAPTER_RANK), MODEL_DIM ** -0.5, 0.109375, ((0, 8),))
    adapter_up = bell_draw(streams_of[8], (ADAPTER_RANK, MODEL_DIM), MODEL_DIM ** -0.5, 0.109375)
    head_tile_reach = draw_head_tile_reach(jax.random.fold_in(streams_of[11], 71), 0)
    key_tile_valid = draw_key_tile_valid(jax.random.fold_in(streams_of[11], 71), 0)
    return dict(queries=queries, keys=keys, values=values, attention_output=attention_output, row_logsumexp=row_logsumexp, output_cotangent=output_cotangent, output_weight=output_weight, adapter_down=adapter_down, adapter_up=adapter_up, head_tile_reach=head_tile_reach, key_tile_valid=key_tile_valid)


adapter_factor = 2.0


def pad_tiles(array):
    widths = ((1, 1), (1, 1), (1, 1)) + ((0, 0),) * (array.ndim - 3)
    return jnp.pad(array, widths)


def tile_at(array, time_pos, height_pos, width_pos):
    first = lax.dynamic_index_in_dim(array, time_pos, 0, False)
    second = lax.dynamic_index_in_dim(first, height_pos, 0, False)
    return lax.dynamic_index_in_dim(second, width_pos, 0, False)


def split_heads(block):
    return block.astype(jnp.float32).reshape(TILE, HEADS, HD)


def round_keep(numbers):
    return lax.optimization_barrier(numbers.astype(jnp.bfloat16)).astype(jnp.float32)


def reference(queries, keys, values, attention_output, row_logsumexp, output_cotangent, output_weight, adapter_down, adapter_up, head_tile_reach, key_tile_valid):
    time_tiles = queries.shape[0]
    height_tiles = queries.shape[1]
    width_tiles = queries.shape[2]
    score_scale = HD ** -0.5
    contract_trailing = (((1,), (1,)), ((), ()))
    contract_leading = (((0,), (0,)), ((), ()))
    flattened_gradient = output_cotangent.reshape(-1, MODEL_DIM)
    mixed_gradient = (adapter_factor * lax.dot_general(flattened_gradient, adapter_up, contract_trailing, preferred_element_type=jnp.float32)).astype(jnp.bfloat16)
    frozen_term = lax.dot_general(flattened_gradient, output_weight, contract_trailing, preferred_element_type=jnp.float32)
    attention_gradient = (frozen_term + lax.dot_general(mixed_gradient, adapter_down, contract_trailing, preferred_element_type=jnp.float32)).astype(jnp.bfloat16)
    flattened_output = attention_output.reshape(-1, ATTENTION_WIDTH)
    adapter_mixed = jnp.dot(flattened_output, adapter_down, preferred_element_type=jnp.float32)
    mixed_halfway = adapter_mixed.astype(jnp.bfloat16)
    grad_a = lax.dot_general(flattened_output, mixed_gradient, contract_leading, preferred_element_type=jnp.float32) / LATENT_TOKENS
    up_map_gradient = adapter_factor * lax.dot_general(mixed_halfway, flattened_gradient, contract_leading, preferred_element_type=jnp.float32) / LATENT_TOKENS
    attention_gradient = attention_gradient.reshape(queries.shape)
    row_delta = jnp.sum((attention_gradient.astype(jnp.float32) * attention_output.astype(jnp.float32)).reshape(time_tiles, height_tiles, width_tiles, TILE, HEADS, HD), axis=-1)
    row_delta = jnp.transpose(row_delta, (0, 1, 2, 4, 3))
    query_pad = pad_tiles(queries)
    key_pad = pad_tiles(keys)
    value_pad = pad_tiles(values)
    dout_pad = pad_tiles(attention_gradient)
    lse_pad = pad_tiles(row_logsumexp)
    delta_pad = pad_tiles(row_delta)
    valid_pad = pad_tiles(key_tile_valid)
    inside_pad = pad_tiles(jnp.ones_like(key_tile_valid))
    reach_time = head_tile_reach[:, 0]
    reach_height = head_tile_reach[:, 1]
    reach_width = head_tile_reach[:, 2]
    plane = height_tiles * width_tiles
    offsets = [(step_time, step_height, step_width) for step_time in (-1, 0, 1) for step_height in (-1, 0, 1) for step_width in (-1, 0, 1)]

    def locate(position):
        time_pos = (position // plane + 1).astype(jnp.int32)
        height_pos = ((position // width_tiles) % height_tiles + 1).astype(jnp.int32)
        width_pos = (position % width_tiles + 1).astype(jnp.int32)
        return time_pos, height_pos, width_pos

    def reach_ok(step_time, step_height, step_width):
        return (abs(step_time) <= reach_time) & (abs(step_height) <= reach_height) & (abs(step_width) <= reach_width)

    def query_tile(position):
        time_pos, height_pos, width_pos = locate(position)
        query_rows = split_heads(tile_at(query_pad, time_pos, height_pos, width_pos))
        grad_rows = split_heads(tile_at(dout_pad, time_pos, height_pos, width_pos))
        lse_rows = tile_at(lse_pad, time_pos, height_pos, width_pos)
        delta_rows = tile_at(delta_pad, time_pos, height_pos, width_pos)
        total = jnp.zeros((TILE, HEADS, HD), jnp.float32)
        for step_time, step_height, step_width in offsets:
            other_time = time_pos + step_time
            other_height = height_pos + step_height
            other_width = width_pos + step_width
            key_rows = split_heads(tile_at(key_pad, other_time, other_height, other_width))
            value_rows = split_heads(tile_at(value_pad, other_time, other_height, other_width))
            linked = (tile_at(valid_pad, other_time, other_height, other_width) == 1) & reach_ok(step_time, step_height, step_width)
            scores = jnp.einsum('qnd,knd->nqk', query_rows, key_rows) * score_scale
            probs = jnp.where(linked[:, None, None], jnp.exp(scores - lse_rows[:, :, None]), 0.0)
            grad_probs = jnp.einsum('qnd,knd->nqk', grad_rows, value_rows)
            dscore = round_keep(probs * (grad_probs - delta_rows[:, :, None]))
            total = total + jnp.einsum('nqk,knd->qnd', dscore, key_rows)
        return (total * score_scale).astype(jnp.bfloat16).reshape(TILE, ATTENTION_WIDTH)

    def key_tile(position):
        time_pos, height_pos, width_pos = locate(position)
        key_rows = split_heads(tile_at(key_pad, time_pos, height_pos, width_pos))
        value_rows = split_heads(tile_at(value_pad, time_pos, height_pos, width_pos))
        key_valid = tile_at(valid_pad, time_pos, height_pos, width_pos) == 1
        total_k = jnp.zeros((TILE, HEADS, HD), jnp.float32)
        total_v = jnp.zeros((TILE, HEADS, HD), jnp.float32)
        for step_time, step_height, step_width in offsets:
            other_time = time_pos + step_time
            other_height = height_pos + step_height
            other_width = width_pos + step_width
            query_rows = split_heads(tile_at(query_pad, other_time, other_height, other_width))
            grad_rows = split_heads(tile_at(dout_pad, other_time, other_height, other_width))
            lse_rows = tile_at(lse_pad, other_time, other_height, other_width)
            delta_rows = tile_at(delta_pad, other_time, other_height, other_width)
            linked = key_valid & (tile_at(inside_pad, other_time, other_height, other_width) == 1) & reach_ok(step_time, step_height, step_width)
            scores = jnp.einsum('qnd,knd->nqk', query_rows, key_rows) * score_scale
            probs = jnp.where(linked[:, None, None], jnp.exp(scores - lse_rows[:, :, None]), 0.0)
            total_v = total_v + jnp.einsum('nqk,qnd->knd', round_keep(probs), grad_rows)
            grad_probs = jnp.einsum('qnd,knd->nqk', grad_rows, value_rows)
            dscore = round_keep(probs * (grad_probs - delta_rows[:, :, None]))
            total_k = total_k + jnp.einsum('nqk,qnd->knd', dscore, query_rows)
        return (total_k * score_scale).astype(jnp.bfloat16).reshape(TILE, ATTENTION_WIDTH), total_v.astype(jnp.bfloat16).reshape(TILE, ATTENTION_WIDTH)

    positions = jnp.arange(time_tiles * plane, dtype=jnp.int32)
    grad_q = lax.map(query_tile, positions).reshape(queries.shape)
    grad_k, grad_v = lax.map(key_tile, positions)
    return grad_q, grad_k.reshape(queries.shape), grad_v.reshape(queries.shape), grad_a, up_map_gradient
```

```python
import functools

import jax
import jax.numpy as jnp
from jax import lax
from jax.experimental import pallas as pl
from jax.experimental.pallas import tpu as pltpu
from jax.sharding import PartitionSpec as P

adapter_factor = 2.0
LOG2E = 1.4426950408889634
FAR = 1e30
MESH = pl.DeviceIdType.MESH
NT = (((1,), (1,)), ((), ()))
TN = (((0,), (0,)), ((), ()))
f32 = jnp.float32
bf16 = jnp.bfloat16


def dot(a, b, dims=(((1,), (0,)), ((), ()))):
    return lax.dot_general(a, b, dims, preferred_element_type=f32)


def kernel(
    sizes,
    q_in,
    k_in,
    v_in,
    o_in,
    lse_in,
    cot_in,
    w_in,
    down_in,
    up_in,
    reach,
    valid,
    gq,
    gk,
    gv,
    ga,
    um,
    qb,
    db,
    st,
    kb,
    vb,
    kt_buf,
    o_v,
    lse_v,
    cot_v,
    w_v,
    down_v,
    up_v,
    dsend,
    stsend,
    dmix,
    dk_acc,
    dv_acc,
    rq,
    ret,
    gq_v,
    dkb,
    dvb,
    mx_own,
    mx,
    px_send,
    px,
    mine,
    red,
    rsb,
    agb,
    fin,
    fx,
    lsem,
    q_send,
    q_recv,
    d_send,
    d_recv,
    s_send,
    s_recv,
    kv_send,
    kv_recv,
    r_send,
    r_recv,
    mx_ssem,
    mx_rsem,
    px_sem,
    rs_ssem,
    rs_rsem,
    ag_ssem,
    ag_rsem,
    fx_sem,
    out_send,
    out_recv,
    out_sem,
):
    tile, hd, t_size, g_size, total_tokens, cols = sizes
    t = lax.axis_index("tm")
    h = lax.axis_index("space")
    g = lax.axis_index("tensor")
    other = 1 - h
    left = lax.rem(t + t_size - 1, t_size)
    right = lax.rem(t + 1, t_size)
    scale = hd**-0.5
    mine_lanes = pl.ds(pl.multiple_of(h * hd, hd), hd)
    other_lanes = pl.ds(pl.multiple_of(other * hd, hd), hd)
    sides = (right, left)
    partner = {"space": other}

    def local(src, dst, index):
        return pltpu.make_async_copy(src, dst, lsem.at[index])

    def remote(src, dst, ssem, rsem, where):
        return pltpu.make_async_remote_copy(
            src_ref=src, dst_ref=dst, send_sem=ssem, recv_sem=rsem, device_id=where, device_id_type=MESH
        )

    def rows_of(w):
        return pl.ds(pl.multiple_of(w * tile, tile), tile)

    loads = [
        local(o_in, o_v, 0),
        local(down_in, down_v, 1),
        local(w_in, w_v, 2),
        local(up_in, up_v, 3),
        local(lse_in, lse_v, 4),
        local(q_in.at[:, mine_lanes], qb.at[h], 5),
        local(k_in.at[:, mine_lanes], kb.at[h], 6),
        local(v_in.at[:, mine_lanes], vb.at[h], 7),
    ]
    for copy in loads[:4]:
        copy.start()
    cot_loads = [local(cot_in.at[rows_of(w)], cot_v.at[rows_of(w)], 8 + w) for w in range(2)]
    for copy in cot_loads + loads[4:]:
        copy.start()

    barrier = pltpu.get_barrier_semaphore()
    for step in range(1, t_size):
        pl.semaphore_signal(
            barrier, inc=1, device_id={"tm": lax.rem(t + step, t_size)}, device_id_type=MESH
        )
    for step in range(1, g_size):
        pl.semaphore_signal(
            barrier, inc=1, device_id={"tensor": lax.rem(g + step, g_size)}, device_id_type=MESH
        )
    for where in (partner, {"tm": left, "space": other}, {"tm": right, "space": other}):
        pl.semaphore_signal(barrier, inc=1, device_id=where, device_id_type=MESH)
    pl.semaphore_wait(barrier, t_size + g_size + 1)

    sends = []
    for side in range(2):
        for n in range(2):
            sends.append(
                remote(
                    q_in.at[:, n * hd : (n + 1) * hd],
                    qb.at[2 + 2 * side + h],
                    q_send.at[side * 2 + n],
                    q_recv.at[2 + 2 * side + h],
                    {"tm": sides[side], "space": n},
                )
            )
    q_pair = remote(q_in.at[:, other_lanes], qb.at[h], q_send.at[4], q_recv.at[h], partner)
    k_pair = remote(k_in.at[:, other_lanes], kb.at[h], kv_send.at[0], kv_recv.at[0], partner)
    v_pair = remote(v_in.at[:, other_lanes], vb.at[h], kv_send.at[1], kv_recv.at[1], partner)
    sends += [q_pair, k_pair, v_pair]
    for copy in sends:
        copy.start()

    loads[0].wait()
    loads[1].wait()
    mixed_part = dot(down_v[...], o_v[...], (((0,), (1,)), ((), ())))
    mx_own[...] = mixed_part.astype(bf16)
    mx_sends = []
    for step in range(1, g_size):
        mx_sends.append(
            remote(
                mx_own,
                mx.at[step - 1],
                mx_ssem.at[step - 1],
                mx_rsem.at[step - 1],
                {"tensor": lax.rem(g + step, g_size)},
            )
        )
    for copy in mx_sends:
        copy.start()

    loads[2].wait()
    loads[3].wait()
    loads[4].wait()

    def grad_sends(w):
        copies = []
        rows = rows_of(w)
        for side in range(2):
            for n in range(2):
                slot = 2 + 2 * side + h
                where = {"tm": sides[side], "space": n}
                index = side * 2 + n
                copies.append(
                    remote(
                        stsend.at[n, w], st.at[slot, w], s_send.at[w, index], s_recv.at[slot, w], where
                    )
                )
                copies.append(
                    remote(
                        dsend.at[n, rows],
                        db.at[slot, rows],
                        d_send.at[w, index],
                        d_recv.at[slot, w],
                        where,
                    )
                )
        copies.append(
            remote(stsend.at[other, w], st.at[h, w], s_send.at[w, 4], s_recv.at[h, w], partner)
        )
        copies.append(
            remote(dsend.at[other, rows], db.at[h, rows], d_send.at[w, 4], d_recv.at[h, w], partner)
        )
        return copies

    def project(w, carry):
        rows = rows_of(w)
        pltpu.make_async_copy(cot_in.at[rows], cot_v.at[rows], lsem.at[8 + w]).wait()
        cot = cot_v[rows, :]
        down_grad = (adapter_factor * dot(cot, up_v[...], NT)).astype(bf16)
        dmix[rows, :] = down_grad
        grad = (dot(cot, w_v[...], NT) + dot(down_grad, down_v[...], NT)).astype(bf16)
        product = (grad.astype(f32) * o_v[rows, :].astype(f32)).T
        for n in range(2):
            delta = jnp.sum(product[n * hd : (n + 1) * hd, :], axis=0, keepdims=True)
            stsend[n, w, 0:1, :] = lse_v[w, n : n + 1, :] * LOG2E
            stsend[n, w, 1:2, :] = delta
            dsend[n, rows, :] = grad[:, n * hd : (n + 1) * hd]
        db[h, rows, :] = dsend[h, rows, :]
        st[h, w] = stsend[h, w]
        for copy in grad_sends(w):
            copy.start()
        return carry

    lax.fori_loop(0, 2, project, 0)

    for copy in mx_sends:
        copy.wait_recv()
    mixed = mx_own[...].astype(f32)
    for step in range(1, g_size):
        mixed += mx[step - 1].astype(f32)
    columns = pl.ds(pl.multiple_of(g * cols, 128), cols)
    up_part = dot(mixed.astype(bf16), cot_v[:, columns]) * (adapter_factor / total_tokens)
    a_part = dot(dmix[...], o_v[...], TN) * (1.0 / total_tokens)
    width = mine.shape[1]
    if width > a_part.shape[1]:
        a_part = jnp.concatenate(
            [a_part, jnp.zeros((a_part.shape[0], width - a_part.shape[1]), f32)], axis=1
        )
    first = h == 0
    mine[...] = jnp.where(first, up_part, a_part)
    px_send[...] = jnp.where(first, a_part, up_part)
    px_copy = remote(px_send, px, px_sem.at[0], px_sem.at[1], partner)
    px_copy.start()

    for copy in loads[5:]:
        copy.wait()
    k_pair.wait_recv()
    v_pair.wait_recv()
    dk_acc[...] = jnp.zeros_like(dk_acc)
    dv_acc[...] = jnp.zeros_like(dv_acc)
    for row in range(2):
        kt_buf[:, row * 2 * tile : (row + 1) * 2 * tile] = kb[row].T

    reach_t = reach[h, 0]
    reach_h = reach[h, 1]
    reach_w = reach[h, 2]

    share = red.shape[1]

    def reduce_sends():
        copies = []
        for step in range(1, t_size):
            peer = lax.rem(t + step, t_size)
            copies.append(
                remote(
                    red.at[peer],
                    rsb.at[step - 1],
                    rs_ssem.at[step - 1],
                    rs_rsem.at[step - 1],
                    {"tm": peer},
                )
            )
        return copies

    def gather_sends():
        copies = []
        for step in range(1, t_size):
            copies.append(
                remote(
                    agb.at[t],
                    agb.at[t],
                    ag_ssem.at[step - 1],
                    ag_rsem.at[step - 1],
                    {"tm": lax.rem(t + step, t_size)},
                )
            )
        return copies

    def locate(u):
        v = u - 4
        near = u < 4
        hq = jnp.where(near, lax.rem(h + u // 2, 2), lax.rem(v // 2 + 2, 2))
        w = jnp.where(near, lax.rem(u, 2), v // 4)
        f = jnp.where(near, 0, 1 + lax.rem(v + 4, 2))
        return near, hq, w, f

    def back(u):
        _, hq, w, f = locate(u)
        rows = rows_of(w)
        where = {"tm": jnp.where(f == 1, left, right), "space": hq}
        slot = jnp.where(f == 1, 1, 0)
        return remote(
            rq.at[u], ret.at[slot, h, rows], r_send.at[u], r_recv.at[slot * 2 + h, w], where
        )

    def back_pair(u):
        _, hq, w, f = locate(u)
        return remote(
            rq.at[u], ret.at[2, h, rows_of(w)], r_send.at[u], r_recv.at[4 + h, w], partner
        )

    def step(u, carry):
        near, hq, w, f = locate(u)
        slot = f * 2 + hq
        rows = rows_of(w)

        @pl.when(u >= 2)
        def _():
            remote(st.at[slot, w], st.at[slot, w], s_send.at[0, 0], s_recv.at[slot, w], partner).wait_recv()
            remote(
                db.at[slot, rows], db.at[slot, rows], d_send.at[0, 0], d_recv.at[slot, w], partner
            ).wait_recv()

        @pl.when((u >= 2) & (w == 0))
        def _():
            remote(qb.at[slot], qb.at[slot], q_send.at[0], q_recv.at[slot], partner).wait_recv()

        @pl.when(u == 4)
        def _():
            px_copy.wait_recv()
            chip = mine[...] + px[...]
            for p in range(t_size):
                red[p] = chip[p * share : (p + 1) * share, :]
            for copy in reduce_sends():
                copy.start()

        @pl.when(u == 8)
        def _():
            for copy in reduce_sends():
                copy.wait_recv()
            total = red[t]
            for index in range(t_size - 1):
                total += rsb[index]
            agb[t] = total
            for copy in gather_sends():
                copy.start()

        q = qb[slot, rows, :]
        d = db[slot, rows, :]
        lse = st[slot, w, 0:1, :]
        delta = st[slot, w, 1:2, :]
        frame = t + jnp.where(f == 0, 0, jnp.where(f == 1, -1, 1))
        frame_ok = (frame >= 0) & (frame < t_size) & (jnp.where(f == 0, 0, 1) <= reach_t)
        dq = None
        for kt in range(4):
            hk, wk = kt // 2, kt % 2
            linked = (
                frame_ok
                & (jnp.abs(hq - hk) <= reach_h)
                & (jnp.abs(w - wk) <= reach_w)
                & (valid[t, hk, wk] == 1)
            )
            shift = lse + jnp.where(linked, 0.0, FAR)
            k = kb[hk, wk * tile : (wk + 1) * tile, :]
            v = vb[hk, wk * tile : (wk + 1) * tile, :]
            probs = jnp.exp2(dot(k, q, NT) * (scale * LOG2E) - shift)
            dprobs = dot(v, d, NT)
            dscore = (probs * (dprobs - delta)).astype(bf16)
            span = slice(kt * tile, (kt + 1) * tile)
            dv_acc[span, :] += dot(probs.astype(bf16), d)
            dk_acc[span, :] += dot(dscore, q)
            part = dot(kt_buf[:, span], dscore)
            dq = part if dq is None else dq + part
        rq[u] = (dq * scale).T.astype(bf16)

        @pl.when(u >= 4)
        def _():
            back(u).start()

        @pl.when((u >= 2) & (u < 4))
        def _():
            back_pair(u).start()

        @pl.when(u < 2)
        def _():
            ret[2, h, rows, :] = rq[u]

        return carry

    lax.fori_loop(0, 12, step, 0)

    for row in range(2):
        dkb[row] = (dk_acc[row * 2 * tile : (row + 1) * 2 * tile, :] * scale).astype(bf16)
        dvb[row] = dv_acc[row * 2 * tile : (row + 1) * 2 * tile, :].astype(bf16)
    pair_out = [
        remote(dkb.at[other], gk.at[:, mine_lanes], out_send.at[0], out_recv.at[0], partner),
        remote(dvb.at[other], gv.at[:, mine_lanes], out_send.at[1], out_recv.at[1], partner),
    ]
    own_out = [
        pltpu.make_async_copy(dkb.at[h], gk.at[:, mine_lanes], out_sem.at[0]),
        pltpu.make_async_copy(dvb.at[h], gv.at[:, mine_lanes], out_sem.at[1]),
    ]
    for copy in pair_out + own_out:
        copy.start()

    gathers = gather_sends()
    for copy in gathers:
        copy.wait_recv()
    for p in range(t_size):
        fin[p * share : (p + 1) * share, :] = agb[p]
    fx_copy = remote(fin, fx, fx_sem.at[0], fx_sem.at[1], partner)
    fx_copy.start()

    for w in range(2):
        rows = rows_of(w)
        for slot in range(4):
            remote(
                ret.at[slot // 2, slot % 2, rows],
                ret.at[slot // 2, slot % 2, rows],
                r_send.at[0],
                r_recv.at[slot, w],
                partner,
            ).wait_recv()
        remote(
            ret.at[2, other, rows], ret.at[2, other, rows], r_send.at[0], r_recv.at[4 + other, w], partner
        ).wait_recv()
        for n in range(2):
            total = (
                ret[0, n, rows, :].astype(f32)
                + ret[1, n, rows, :].astype(f32)
                + ret[2, n, rows, :].astype(f32)
            )
            gq_v[rows, n * hd : (n + 1) * hd] = total.astype(bf16)
    gq_copy = pltpu.make_async_copy(gq_v, gq, out_sem.at[2])
    gq_copy.start()

    fx_copy.wait_recv()
    um[...] = jnp.where(first, fin[...], fx[...])[:, :cols]
    ga[...] = jnp.where(first, fx[...], fin[...])[:, : ga.shape[0]].T

    for copy in sends + mx_sends + [px_copy, fx_copy] + pair_out + gathers + reduce_sends():
        copy.wait_send()
    for w in range(2):
        for copy in grad_sends(w):
            copy.wait_send()

    def drain(u, carry):
        back(u).wait_send()
        return carry

    lax.fori_loop(4, 12, drain, 0)
    for u in (2, 3):
        back_pair(u).wait_send()
    for copy in pair_out:
        copy.wait_recv()
    for copy in own_out + [gq_copy]:
        copy.wait()


def body(
    queries,
    keys,
    values,
    attention_output,
    row_logsumexp,
    output_cotangent,
    output_weight,
    adapter_down,
    adapter_up,
    head_tile_reach,
    key_tile_valid,
):
    tile = queries.shape[3]
    features = queries.shape[4]
    tokens = queries.shape[2] * tile
    heads = head_tile_reach.shape[0]
    hd = features // heads
    rank = adapter_down.shape[1]
    model = output_cotangent.shape[4]
    t_size = lax.axis_size("tm")
    g_size = lax.axis_size("tensor")
    total_tokens = t_size * lax.axis_size("space") * tokens
    cols = model // g_size
    width = max(cols, features)
    share = rank // t_size
    sizes = (tile, hd, t_size, g_size, total_tokens, cols)

    def flat(array):
        return array.reshape(tokens, array.shape[-1])

    anywhere = pl.BlockSpec(memory_space=pl.ANY)
    vmem = pl.BlockSpec(memory_space=pltpu.VMEM)
    smem = pl.BlockSpec(memory_space=pltpu.SMEM)
    dma = pltpu.SemaphoreType.DMA
    grads = jax.ShapeDtypeStruct((tokens, features), bf16)
    scratch = [
        pltpu.VMEM((6, tokens, hd), bf16),
        pltpu.VMEM((6, tokens, hd), bf16),
        pltpu.VMEM((6, 2, 8, tile), f32),
        pltpu.VMEM((2, tokens, hd), bf16),
        pltpu.VMEM((2, tokens, hd), bf16),
        pltpu.VMEM((hd, 2 * tokens), bf16),
        pltpu.VMEM((tokens, features), bf16),
        pltpu.VMEM((2, heads, tile), f32),
        pltpu.VMEM((tokens, model), bf16),
        pltpu.VMEM((features, model), bf16),
        pltpu.VMEM((features, rank), bf16),
        pltpu.VMEM((rank, model), bf16),
        pltpu.VMEM((2, tokens, hd), bf16),
        pltpu.VMEM((2, 2, 8, tile), f32),
        pltpu.VMEM((tokens, rank), bf16),
        pltpu.VMEM((2 * tokens, hd), f32),
        pltpu.VMEM((2 * tokens, hd), f32),
        pltpu.VMEM((12, tile, hd), bf16),
        pltpu.VMEM((3, 2, tokens, hd), bf16),
        pltpu.VMEM((tokens, features), bf16),
        pltpu.VMEM((2, tokens, hd), bf16),
        pltpu.VMEM((2, tokens, hd), bf16),
        pltpu.VMEM((rank, tokens), bf16),
        pltpu.VMEM((g_size - 1, rank, tokens), bf16),
        pltpu.VMEM((rank, width), f32),
        pltpu.VMEM((rank, width), f32),
        pltpu.VMEM((rank, width), f32),
        pltpu.VMEM((t_size, share, width), f32),
        pltpu.VMEM((t_size - 1, share, width), f32),
        pltpu.VMEM((t_size, share, width), f32),
        pltpu.VMEM((rank, width), f32),
        pltpu.VMEM((rank, width), f32),
        dma((10,)),
        dma((5,)),
        dma((6,)),
        dma((2, 5)),
        dma((6, 2)),
        dma((2, 5)),
        dma((6, 2)),
        dma((2,)),
        dma((2,)),
        dma((12,)),
        dma((6, 2)),
        dma((g_size - 1,)),
        dma((g_size - 1,)),
        dma((2,)),
        dma((t_size - 1,)),
        dma((t_size - 1,)),
        dma((t_size - 1,)),
        dma((t_size - 1,)),
        dma((2,)),
        dma((2,)),
        dma((2,)),
        dma((3,)),
    ]
    grad_q, grad_k, grad_v, grad_a, up_map_gradient = pl.pallas_call(
        functools.partial(kernel, sizes),
        out_shape=(
            grads,
            grads,
            grads,
            jax.ShapeDtypeStruct((features, rank), f32),
            jax.ShapeDtypeStruct((rank, cols), f32),
        ),
        in_specs=[anywhere] * 9 + [smem] * 2,
        out_specs=(anywhere, anywhere, anywhere, vmem, vmem),
        scratch_shapes=scratch,
        compiler_params=pltpu.CompilerParams(
            collective_id=0, has_side_effects=True, vmem_limit_bytes=48 * 1024 * 1024
        ),
    )(
        flat(queries),
        flat(keys),
        flat(values),
        flat(attention_output),
        row_logsumexp.reshape(row_logsumexp.shape[2:]),
        flat(output_cotangent),
        output_weight,
        adapter_down,
        adapter_up,
        head_tile_reach,
        key_tile_valid,
    )
    return (
        grad_q.reshape(queries.shape),
        grad_k.reshape(queries.shape),
        grad_v.reshape(queries.shape),
        grad_a,
        up_map_gradient,
    )


def solution(mesh):
    placed = (
        P("tm", "space", None, None, "tensor"),
        P("tm", "space", None, None, "tensor"),
        P("tm", "space", None, None, "tensor"),
        P("tm", "space", None, None, "tensor"),
        P("tm", "space", None, "tensor", None),
        P("tm", "space", None, None, None),
        P("tensor", None),
        P("tensor", None),
        P(),
        P("tensor", None),
        P(),
    )
    return jax.shard_map(
        body,
        mesh=mesh,
        in_specs=placed,
        out_specs=(
            P("tm", "space", None, None, "tensor"),
            P("tm", "space", None, None, "tensor"),
            P("tm", "space", None, None, "tensor"),
            P("tensor", None),
            P(None, "tensor"),
        ),
        check_vma=False,
    )
```

```python
import functools

import jax
import jax.numpy as jnp
from jax import lax
from jax.experimental import pallas as pl
from jax.experimental.pallas import tpu as pltpu
from jax.sharding import PartitionSpec as P

adapter_factor = 2.0
LOG2E = 1.4426950408889634
FAR = 1e30
MESH = pl.DeviceIdType.MESH
NT = (((1,), (1,)), ((), ()))
TN = (((0,), (0,)), ((), ()))
f32 = jnp.float32
bf16 = jnp.bfloat16


def dot(a, b, dims=(((1,), (0,)), ((), ()))):
    return lax.dot_general(a, b, dims, preferred_element_type=f32)


def kernel(
    sizes,
    q_in,
    k_in,
    v_in,
    o_in,
    lse_in,
    cot_in,
    w_in,
    down_in,
    up_in,
    reach_in,
    valid_in,
    gq,
    gk,
    gv,
    ga,
    um,
    qb,
    db,
    st,
    kb,
    vb,
    kt_buf,
    o_v,
    lse_v,
    cot_v,
    w_v,
    down_v,
    up_v,
    dsend,
    stsend,
    dmix,
    dk_acc,
    dv_acc,
    rq,
    ret,
    gq_v,
    dkb,
    dvb,
    mx_own,
    mx,
    pa,
    pb,
    ra,
    rb,
    zb,
    fq,
    reach,
    valid,
    lsem,
    q_send,
    q_recv,
    d_send,
    d_recv,
    s_send,
    s_recv,
    kv_send,
    kv_recv,
    r_send,
    r_recv,
    mx_ssem,
    mx_rsem,
    oc_ssem,
    oc_rsem,
    z_ssem,
    z_rsem,
    f_ssem,
    f_rsem,
    out_send,
    out_recv,
    out_sem,
):
    tile, hd, t_size, g_size, total_tokens, cols = sizes
    t = lax.axis_index("tm")
    h = lax.axis_index("space")
    g = lax.axis_index("tensor")
    other = 1 - h
    left = lax.rem(t + t_size - 1, t_size)
    right = lax.rem(t + 1, t_size)
    z_size = t_size // 2
    y_size = g_size // 2
    x_lo = t // z_size
    z = lax.rem(t, z_size)
    y = g // 2
    x_hi = lax.rem(g, 2)
    quarter = 2 * x_lo + h
    scale = hd**-0.5
    mine_lanes = pl.ds(pl.multiple_of(h * hd, hd), hd)
    other_lanes = pl.ds(pl.multiple_of(other * hd, hd), hd)

    def quad(step):
        peer = lax.rem(quarter + step, 4)
        return peer, {"tm": lax.rem(peer // 2, 2) * z_size + z, "space": lax.rem(peer, 2)}

    sides = (right, left)
    partner = {"space": other}

    def local(src, dst, index):
        return pltpu.make_async_copy(src, dst, lsem.at[index])

    def remote(src, dst, ssem, rsem, where):
        return pltpu.make_async_remote_copy(
            src_ref=src, dst_ref=dst, send_sem=ssem, recv_sem=rsem, device_id=where, device_id_type=MESH
        )

    def rows_of(w):
        return pl.ds(pl.multiple_of(w * tile, tile), tile)

    loads = [
        local(o_in, o_v, 0),
        local(down_in, down_v, 1),
        local(w_in, w_v, 2),
        local(up_in, up_v, 3),
        local(lse_in, lse_v, 4),
        local(q_in.at[:, mine_lanes], qb.at[h], 5),
        local(k_in.at[:, mine_lanes], kb.at[h], 6),
        local(v_in.at[:, mine_lanes], vb.at[h], 7),
        local(reach_in, reach, 10),
        local(valid_in, valid, 11),
    ]
    for copy in loads[:4]:
        copy.start()
    cot_loads = [local(cot_in.at[rows_of(w)], cot_v.at[rows_of(w)], 8 + w) for w in range(2)]
    for copy in cot_loads + loads[4:]:
        copy.start()

    barrier = pltpu.get_barrier_semaphore()
    greeted = [{"tm": side, "space": n} for side in (left, right) for n in range(2)]
    greeted += [{"tensor": lax.rem(y + step, y_size) * 2 + x_hi} for step in range(1, y_size)]
    greeted += [quad(step)[1] for step in range(1, 4)]
    greeted += [{**quad(step)[1], "tensor": 2 * y + 1 - x_hi} for step in range(4)]
    greeted += [{"tm": x_lo * z_size + lax.rem(z + step, z_size)} for step in range(1, z_size)]
    for where in greeted:
        pl.semaphore_signal(barrier, inc=1, device_id=where, device_id_type=MESH)
    pl.semaphore_wait(barrier, len(greeted))

    sends = []
    for side in range(2):
        for n in range(2):
            sends.append(
                remote(
                    q_in.at[:, n * hd : (n + 1) * hd],
                    qb.at[2 + 2 * side + h],
                    q_send.at[side * 2 + n],
                    q_recv.at[2 + 2 * side + h],
                    {"tm": sides[side], "space": n},
                )
            )
    q_pair = remote(q_in.at[:, other_lanes], qb.at[h], q_send.at[4], q_recv.at[h], partner)
    k_pair = remote(k_in.at[:, other_lanes], kb.at[h], kv_send.at[0], kv_recv.at[0], partner)
    v_pair = remote(v_in.at[:, other_lanes], vb.at[h], kv_send.at[1], kv_recv.at[1], partner)
    sends += [q_pair, k_pair, v_pair]
    for copy in sends:
        copy.start()

    loads[0].wait()
    loads[1].wait()
    mixed_part = dot(down_v[...], o_v[...], NT)
    mx_own[...] = mixed_part.astype(bf16)
    mx_sends = []
    for step in range(1, y_size):
        mx_sends.append(
            remote(
                mx_own,
                mx.at[step - 1],
                mx_ssem.at[step - 1],
                mx_rsem.at[step - 1],
                {"tensor": lax.rem(y + step, y_size) * 2 + x_hi},
            )
        )
    for copy in mx_sends:
        copy.start()

    loads[2].wait()
    loads[3].wait()
    loads[4].wait()

    def grad_sends(w):
        copies = []
        rows = rows_of(w)
        for side in range(2):
            for n in range(2):
                slot = 2 + 2 * side + h
                where = {"tm": sides[side], "space": n}
                index = side * 2 + n
                copies.append(
                    remote(
                        stsend.at[n, w], st.at[slot, w], s_send.at[w, index], s_recv.at[slot, w], where
                    )
                )
                copies.append(
                    remote(
                        dsend.at[n, rows],
                        db.at[slot, rows],
                        d_send.at[w, index],
                        d_recv.at[slot, w],
                        where,
                    )
                )
        copies.append(
            remote(stsend.at[other, w], st.at[h, w], s_send.at[w, 4], s_recv.at[h, w], partner)
        )
        copies.append(
            remote(dsend.at[other, rows], db.at[h, rows], d_send.at[w, 4], d_recv.at[h, w], partner)
        )
        return copies

    def project(w, carry):
        rows = rows_of(w)
        pltpu.make_async_copy(cot_in.at[rows], cot_v.at[rows], lsem.at[8 + w]).wait()
        cot = cot_v[rows, :]
        down_grad = (adapter_factor * dot(cot, up_v[...], NT)).astype(bf16)
        dmix[rows, :] = down_grad
        grad = (dot(cot, w_v[...], NT) + dot(down_grad, down_v[...])).astype(bf16)
        product = (grad.astype(f32) * o_v[rows, :].astype(f32)).T
        for n in range(2):
            delta = jnp.sum(product[n * hd : (n + 1) * hd, :], axis=0, keepdims=True)
            stsend[n, w, 0:1, :] = lse_v[w, n : n + 1, :] * LOG2E
            stsend[n, w, 1:2, :] = delta
            dsend[n, rows, :] = grad[:, n * hd : (n + 1) * hd]
        db[h, rows, :] = dsend[h, rows, :]
        st[h, w] = stsend[h, w]
        for copy in grad_sends(w):
            copy.start()
        return carry

    lax.fori_loop(0, 2, project, 0)

    ranks = pa.shape[1]
    features = ga.shape[1]
    oct_sends = []
    for step in range(4):
        peer, where = quad(step)
        if step:
            oct_sends.append(
                remote(
                    pa.at[peer], ra.at[step - 1], oc_ssem.at[step - 1], oc_rsem.at[step - 1], where
                )
            )
        oct_sends.append(
            remote(
                pb.at[peer],
                rb.at[step],
                oc_ssem.at[3 + step],
                oc_rsem.at[3 + step],
                {**where, "tensor": 2 * y + 1 - x_hi},
            )
        )
    z_sends = []
    for step in range(1, z_size):
        z_sends.append(
            remote(
                zb.at[z],
                zb.at[z],
                z_ssem.at[step - 1],
                z_rsem.at[step - 1],
                {"tm": x_lo * z_size + lax.rem(z + step, z_size)},
            )
        )
    quad_sends = []
    for step in range(1, 4):
        quad_sends.append(
            remote(
                fq.at[quarter], fq.at[quarter], f_ssem.at[step - 1], f_rsem.at[step - 1], quad(step)[1]
            )
        )

    def adapter_parts():
        for copy in mx_sends:
            copy.wait_recv()
        mixed = mx_own[...].astype(f32)
        for index in range(y_size - 1):
            mixed += mx[index].astype(f32)
        mixed = mixed.astype(bf16)
        parts = []
        for side in range(2):
            columns = pl.ds(pl.multiple_of((2 * y + side) * cols, 128), cols)
            parts.append(dot(mixed, cot_v[:, columns]) * (adapter_factor / total_tokens))
        a_part = dot(dmix[...], o_v[...], TN) * (1.0 / total_tokens)
        first = x_hi == 0
        same = jnp.where(first, parts[0], parts[1])
        across = jnp.where(first, parts[1], parts[0])
        for p in range(4):
            rows = slice(p * ranks, (p + 1) * ranks)
            pa[p, :, :cols] = same[rows, :]
            pa[p, :, cols:] = a_part[rows, :]
            pb[p] = across[rows, :]
        for copy in oct_sends:
            copy.start()

    def adapter_z():
        for copy in oct_sends:
            copy.wait_recv()
        total = pa[quarter]
        for index in range(3):
            total += ra[index]
        up_total = total[:, :cols]
        for index in range(4):
            up_total += rb[index]
        zb[z, :ranks, :cols] = up_total.astype(bf16)
        zb[z, ranks:, :features] = total[:, cols:].astype(bf16)
        for copy in z_sends:
            copy.start()

    def adapter_quad():
        for copy in z_sends:
            copy.wait_recv()
        total = zb[0].astype(f32)
        for index in range(1, z_size):
            total += zb[index].astype(f32)
        fq[quarter] = total
        for copy in quad_sends:
            copy.start()

    def adapter_out():
        for copy in quad_sends:
            copy.wait_recv()
        for p in range(4):
            rows = slice(p * ranks, (p + 1) * ranks)
            um[rows, :] = fq[p, :ranks, :cols]
            ga[rows, :] = fq[p, ranks:, :features]

    zb[z] = jnp.zeros(zb.shape[1:], bf16)

    for copy in loads[5:]:
        copy.wait()
    k_pair.wait_recv()
    v_pair.wait_recv()
    dk_acc[...] = jnp.zeros_like(dk_acc)
    dv_acc[...] = jnp.zeros_like(dv_acc)
    for row in range(2):
        kt_buf[:, row * 2 * tile : (row + 1) * 2 * tile] = kb[row].T

    reach_t = reach[h, 0]
    reach_h = reach[h, 1]
    reach_w = reach[h, 2]

    def locate(u):
        v = u - 2
        near = u < 2
        w = jnp.where(near, u, v // 2)
        f = jnp.where(near, 0, 1 + lax.rem(v + 2, 2))
        return near, w, f

    def back(u, hq):
        _, w, f = locate(u)
        rows = rows_of(w)
        where = {"tm": jnp.where(f == 1, left, right), "space": hq}
        slot = jnp.where(f == 1, 1, 0)
        return remote(
            rq.at[u, hq], ret.at[slot, h, rows], r_send.at[u, hq], r_recv.at[slot * 2 + h, w], where
        )

    def back_pair(u):
        rows = rows_of(u)
        return remote(
            rq.at[u, other], ret.at[2, h, rows], r_send.at[u, other], r_recv.at[4 + h, u], partner
        )

    def arrive(slot, w):
        rows = rows_of(w)
        remote(st.at[slot, w], st.at[slot, w], s_send.at[0, 0], s_recv.at[slot, w], partner).wait_recv()
        remote(
            db.at[slot, rows], db.at[slot, rows], d_send.at[0, 0], d_recv.at[slot, w], partner
        ).wait_recv()

        @pl.when(w == 0)
        def _():
            remote(qb.at[slot], qb.at[slot], q_send.at[0], q_recv.at[slot], partner).wait_recv()

    def step(u, carry):
        near, w, f = locate(u)
        rows = rows_of(w)

        @pl.when(near)
        def _():
            arrive(other, w)

        @pl.when(u == 1)
        def _():
            adapter_parts()

        @pl.when(u == 3)
        def _():
            adapter_z()

        @pl.when(u >= 2)
        def _():
            for hq in range(2):
                arrive(2 * f + hq, w)

        q = jnp.concatenate([qb[2 * f, rows, :], qb[2 * f + 1, rows, :]], axis=0)
        d = jnp.concatenate([db[2 * f, rows, :], db[2 * f + 1, rows, :]], axis=0)
        lse = [st[2 * f + hq, w, 0:1, :] for hq in range(2)]
        delta = jnp.concatenate([st[2 * f + hq, w, 1:2, :] for hq in range(2)], axis=1)
        frame = t + jnp.where(f == 0, 0, jnp.where(f == 1, -1, 1))
        frame_ok = (frame >= 0) & (frame < t_size) & (jnp.where(f == 0, 0, 1) <= reach_t)
        dq = None
        for kt in range(4):
            hk, wk = kt // 2, kt % 2
            key_ok = frame_ok & (jnp.abs(w - wk) <= reach_w) & (valid[hk, wk, t] == 1)
            shift = jnp.concatenate(
                [
                    lse[hq] + jnp.where(key_ok & (abs(hq - hk) <= reach_h), 0.0, FAR)
                    for hq in range(2)
                ],
                axis=1,
            )
            k = kb[hk, wk * tile : (wk + 1) * tile, :]
            v = vb[hk, wk * tile : (wk + 1) * tile, :]
            probs = jnp.exp2(dot(k, q, NT) * (scale * LOG2E) - shift)
            dprobs = dot(v, d, NT)
            dscore = (probs * (dprobs - delta)).astype(bf16)
            span = slice(kt * tile, (kt + 1) * tile)
            dv_acc[span, :] += dot(probs.astype(bf16), d)
            dk_acc[span, :] += dot(dscore, q)
            part = dot(kt_buf[:, span], dscore)
            dq = part if dq is None else dq + part
        dq_rows = (dq * scale).T.astype(bf16)
        for hq in range(2):
            rq[u, hq] = dq_rows[hq * tile : (hq + 1) * tile, :]

        @pl.when(u >= 2)
        def _():
            for hq in range(2):
                back(u, hq).start()

        @pl.when(near)
        def _():
            back_pair(u).start()
            ret[2, h, rows, :] = rq[u, h]

        return carry

    lax.fori_loop(0, 6, step, 0)

    for row in range(2):
        dkb[row] = (dk_acc[row * 2 * tile : (row + 1) * 2 * tile, :] * scale).astype(bf16)
        dvb[row] = dv_acc[row * 2 * tile : (row + 1) * 2 * tile, :].astype(bf16)
    pair_out = [
        remote(dkb.at[other], gk.at[:, mine_lanes], out_send.at[0], out_recv.at[0], partner),
        remote(dvb.at[other], gv.at[:, mine_lanes], out_send.at[1], out_recv.at[1], partner),
    ]
    own_out = [
        pltpu.make_async_copy(dkb.at[h], gk.at[:, mine_lanes], out_sem.at[0]),
        pltpu.make_async_copy(dvb.at[h], gv.at[:, mine_lanes], out_sem.at[1]),
    ]
    for copy in pair_out + own_out:
        copy.start()

    adapter_quad()

    for w in range(2):
        rows = rows_of(w)
        for slot in range(4):
            remote(
                ret.at[slot // 2, slot % 2, rows],
                ret.at[slot // 2, slot % 2, rows],
                r_send.at[0],
                r_recv.at[slot, w],
                partner,
            ).wait_recv()
        remote(
            ret.at[2, other, rows], ret.at[2, other, rows], r_send.at[0], r_recv.at[4 + other, w], partner
        ).wait_recv()
        for n in range(2):
            total = (
                ret[0, n, rows, :].astype(f32)
                + ret[1, n, rows, :].astype(f32)
                + ret[2, n, rows, :].astype(f32)
            )
            gq_v[rows, n * hd : (n + 1) * hd] = total.astype(bf16)
    gq_copy = pltpu.make_async_copy(gq_v, gq, out_sem.at[2])
    gq_copy.start()

    adapter_out()

    for copy in sends + mx_sends + oct_sends + z_sends + quad_sends + pair_out:
        copy.wait_send()
    for w in range(2):
        for copy in grad_sends(w):
            copy.wait_send()

    def drain(u, carry):
        for hq in range(2):
            back(u, hq).wait_send()
        return carry

    lax.fori_loop(2, 6, drain, 0)
    for u in range(2):
        back_pair(u).wait_send()
    for copy in pair_out:
        copy.wait_recv()
    for copy in own_out + [gq_copy]:
        copy.wait()


def finish(*refs):
    count = len(refs) // 2
    for index in range(count):
        refs[count + index][...] = refs[index][...]


def body(
    queries,
    keys,
    values,
    attention_output,
    row_logsumexp,
    output_cotangent,
    output_weight,
    adapter_down,
    adapter_up,
    head_tile_reach,
    key_tile_valid,
):
    tile = queries.shape[3]
    features = queries.shape[4]
    tokens = queries.shape[2] * tile
    heads = head_tile_reach.shape[0]
    hd = features // heads
    rank = adapter_down.shape[1]
    model = output_cotangent.shape[4]
    t_size = lax.axis_size("tm")
    g_size = lax.axis_size("tensor")
    total_tokens = t_size * lax.axis_size("space") * tokens
    cols = model // g_size
    width = max(cols, features)
    ranks = rank // 4
    y_size = g_size // 2
    sizes = (tile, hd, t_size, g_size, total_tokens, cols)

    def flat(array):
        return array.reshape(tokens, array.shape[-1])

    anywhere = pl.BlockSpec(memory_space=pl.ANY)
    hbm = pl.BlockSpec(memory_space=pltpu.HBM)
    vmem = pl.BlockSpec(memory_space=pltpu.VMEM)
    smem = pl.BlockSpec(memory_space=pltpu.SMEM)
    dma = pltpu.SemaphoreType.DMA
    grads = jax.ShapeDtypeStruct((tokens, features), bf16)
    scratch = [
        pltpu.VMEM((6, tokens, hd), bf16),
        pltpu.VMEM((6, tokens, hd), bf16),
        pltpu.VMEM((6, 2, 8, tile), f32),
        pltpu.VMEM((2, tokens, hd), bf16),
        pltpu.VMEM((2, tokens, hd), bf16),
        pltpu.VMEM((hd, 2 * tokens), bf16),
        pltpu.VMEM((tokens, features), bf16),
        pltpu.VMEM((2, heads, tile), f32),
        pltpu.VMEM((tokens, model), bf16),
        pltpu.VMEM((features, model), bf16),
        pltpu.VMEM((rank, features), bf16),
        pltpu.VMEM((rank, model), bf16),
        pltpu.VMEM((2, tokens, hd), bf16),
        pltpu.VMEM((2, 2, 8, tile), f32),
        pltpu.VMEM((tokens, rank), bf16),
        pltpu.VMEM((2 * tokens, hd), f32),
        pltpu.VMEM((2 * tokens, hd), f32),
        pltpu.VMEM((6, 2, tile, hd), bf16),
        pltpu.VMEM((3, 2, tokens, hd), bf16),
        pltpu.VMEM((tokens, features), bf16),
        pltpu.VMEM((2, tokens, hd), bf16),
        pltpu.VMEM((2, tokens, hd), bf16),
        pltpu.VMEM((rank, tokens), bf16),
        pltpu.VMEM((max(y_size - 1, 1), rank, tokens), bf16),
        pltpu.VMEM((4, ranks, cols + features), f32),
        pltpu.VMEM((4, ranks, cols), f32),
        pltpu.VMEM((3, ranks, cols + features), f32),
        pltpu.VMEM((4, ranks, cols), f32),
        pltpu.VMEM((t_size // 2, 2 * ranks, width), bf16),
        pltpu.VMEM((4, 2 * ranks, width), f32),
        pltpu.SMEM(head_tile_reach.shape, jnp.int32),
        pltpu.SMEM(key_tile_valid.shape[1:] + key_tile_valid.shape[:1], jnp.int32),
        dma((12,)),
        dma((5,)),
        dma((6,)),
        dma((2, 5)),
        dma((6, 2)),
        dma((2, 5)),
        dma((6, 2)),
        dma((2,)),
        dma((2,)),
        dma((6, 2)),
        dma((6, 2)),
        dma((max(y_size - 1, 1),)),
        dma((max(y_size - 1, 1),)),
        dma((7,)),
        dma((7,)),
        dma((t_size // 2 - 1,)),
        dma((t_size // 2 - 1,)),
        dma((3,)),
        dma((3,)),
        dma((2,)),
        dma((2,)),
        dma((3,)),
    ]
    results = pl.pallas_call(
        functools.partial(kernel, sizes),
        out_shape=(
            grads,
            grads,
            grads,
            jax.ShapeDtypeStruct((rank, features), f32),
            jax.ShapeDtypeStruct((rank, cols), f32),
        ),
        in_specs=[hbm] * 11,
        out_specs=(anywhere, anywhere, anywhere, vmem, vmem),
        scratch_shapes=scratch,
        compiler_params=pltpu.CompilerParams(
            collective_id=0, has_side_effects=True, vmem_limit_bytes=62 * 1024 * 1024
        ),
    )(
        flat(queries),
        flat(keys),
        flat(values),
        flat(attention_output),
        row_logsumexp.reshape(row_logsumexp.shape[2:]),
        flat(output_cotangent),
        output_weight,
        adapter_down.T,
        adapter_up,
        head_tile_reach,
        jnp.transpose(key_tile_valid, (1, 2, 0)),
    )
    grad_q, grad_k, grad_v, grad_a, up_map_gradient = pl.pallas_call(
        finish,
        out_shape=tuple(jax.ShapeDtypeStruct(array.shape, array.dtype) for array in results),
        in_specs=[vmem] * 5,
        out_specs=(vmem,) * 5,
        compiler_params=pltpu.CompilerParams(vmem_limit_bytes=62 * 1024 * 1024),
    )(*results)
    return (
        grad_q.reshape(queries.shape),
        grad_k.reshape(queries.shape),
        grad_v.reshape(queries.shape),
        grad_a.T,
        up_map_gradient,
    )


def solution(mesh):
    placed = (
        P("tm", "space", None, None, "tensor"),
        P("tm", "space", None, None, "tensor"),
        P("tm", "space", None, None, "tensor"),
        P("tm", "space", None, None, "tensor"),
        P("tm", "space", None, "tensor", None),
        P("tm", "space", None, None, None),
        P("tensor", None),
        P("tensor", None),
        P(),
        P("tensor", None),
        P(),
    )
    return jax.shard_map(
        body,
        mesh=mesh,
        in_specs=placed,
        out_specs=(
            P("tm", "space", None, None, "tensor"),
            P("tm", "space", None, None, "tensor"),
            P("tm", "space", None, None, "tensor"),
            P("tensor", None),
            P(None, "tensor"),
        ),
        check_vma=False,
    )
```

```python
import functools

import jax
import jax.numpy as jnp
from jax import lax
from jax.experimental import pallas as pl
from jax.experimental.pallas import tpu as pltpu
from jax.sharding import PartitionSpec as P

adapter_factor = 2.0
LOG2E = 1.4426950408889634
FAR = 1e30
MESH = pl.DeviceIdType.MESH
NT = (((1,), (1,)), ((), ()))
TN = (((0,), (0,)), ((), ()))
f32 = jnp.float32
bf16 = jnp.bfloat16


def dot(a, b, dims=(((1,), (0,)), ((), ()))):
    return lax.dot_general(a, b, dims, preferred_element_type=f32)


def kernel(
    sizes,
    q_in,
    k_in,
    v_in,
    o_in,
    lse_in,
    cot_in,
    w_in,
    down_in,
    up_in,
    reach_in,
    valid_in,
    gq,
    gk,
    gv,
    ga,
    um,
    qb,
    db,
    st,
    kb,
    vb,
    kt_buf,
    o_v,
    lse_v,
    cot_v,
    w_v,
    down_v,
    up_v,
    dsend,
    stsend,
    dmix,
    dk_acc,
    dv_acc,
    rq,
    ret,
    gq_v,
    dkb,
    dvb,
    mx_own,
    mx,
    pa,
    pb,
    ra,
    rb,
    zb,
    fq,
    reach,
    valid,
    lsem,
    q_send,
    q_recv,
    d_send,
    d_recv,
    s_send,
    s_recv,
    kv_send,
    kv_recv,
    r_send,
    r_recv,
    mx_ssem,
    mx_rsem,
    oc_ssem,
    oc_rsem,
    z_ssem,
    z_rsem,
    f_ssem,
    f_rsem,
    out_send,
    out_recv,
    out_sem,
):
    tile, hd, t_size, g_size, total_tokens, cols = sizes
    t = lax.axis_index("tm")
    h = lax.axis_index("space")
    g = lax.axis_index("tensor")
    other = 1 - h
    left = lax.rem(t + t_size - 1, t_size)
    right = lax.rem(t + 1, t_size)
    z_size = t_size // 2
    y_size = g_size // 2
    x_lo = t // z_size
    z = lax.rem(t, z_size)
    y = g // 2
    x_hi = lax.rem(g, 2)
    quarter = 2 * x_lo + h
    scale = hd**-0.5
    mine_lanes = pl.ds(pl.multiple_of(h * hd, hd), hd)
    other_lanes = pl.ds(pl.multiple_of(other * hd, hd), hd)

    def quad(step):
        peer = lax.rem(quarter + step, 4)
        return peer, {"tm": lax.rem(peer // 2, 2) * z_size + z, "space": lax.rem(peer, 2)}

    sides = (right, left)
    partner = {"space": other}
    has = (t < t_size - 1, t > 0)

    def local(src, dst, index):
        return pltpu.make_async_copy(src, dst, lsem.at[index])

    def remote(src, dst, ssem, rsem, where):
        return pltpu.make_async_remote_copy(
            src_ref=src, dst_ref=dst, send_sem=ssem, recv_sem=rsem, device_id=where, device_id_type=MESH
        )

    def rows_of(w):
        return pl.ds(pl.multiple_of(w * tile, tile), tile)

    loads = [
        local(o_in, o_v, 0),
        local(down_in, down_v, 1),
        local(w_in, w_v, 2),
        local(up_in, up_v, 3),
        local(lse_in, lse_v, 4),
        local(q_in.at[:, mine_lanes], qb.at[h], 5),
        local(k_in.at[:, mine_lanes], kb.at[h], 6),
        local(v_in.at[:, mine_lanes], vb.at[h], 7),
        local(reach_in, reach, 10),
        local(valid_in, valid, 11),
    ]
    for copy in loads[:4]:
        copy.start()
    cot_loads = [local(cot_in.at[rows_of(w)], cot_v.at[rows_of(w)], 8 + w) for w in range(2)]
    for copy in cot_loads + loads[4:]:
        copy.start()

    barrier = pltpu.get_barrier_semaphore()
    greeted = [{"tm": side, "space": n} for side in (left, right) for n in range(2)]
    greeted += [{"tensor": lax.rem(y + step, y_size) * 2 + x_hi} for step in range(1, y_size)]
    greeted += [quad(step)[1] for step in range(1, 4)]
    greeted += [{**quad(step)[1], "tensor": 2 * y + 1 - x_hi} for step in range(4)]
    greeted += [{"tm": x_lo * z_size + lax.rem(z + step, z_size)} for step in range(1, z_size)]
    for where in greeted:
        pl.semaphore_signal(barrier, inc=1, device_id=where, device_id_type=MESH)
    loads[0].wait()
    loads[1].wait()
    mixed_part = dot(down_v[...], o_v[...], NT)
    mx_own[...] = mixed_part.astype(bf16)

    pl.semaphore_wait(barrier, len(greeted))

    mx_sends = []
    for step in range(1, y_size):
        mx_sends.append(
            remote(
                mx_own,
                mx.at[step - 1],
                mx_ssem.at[step - 1],
                mx_rsem.at[step - 1],
                {"tensor": lax.rem(y + step, y_size) * 2 + x_hi},
            )
        )
    for copy in mx_sends:
        copy.start()

    def q_sends(side):
        return [
            remote(
                q_in.at[:, n * hd : (n + 1) * hd],
                qb.at[2 + 2 * side + h],
                q_send.at[side * 2 + n],
                q_recv.at[2 + 2 * side + h],
                {"tm": sides[side], "space": n},
            )
            for n in range(2)
        ]

    q_pair = remote(q_in.at[:, other_lanes], qb.at[h], q_send.at[4], q_recv.at[h], partner)
    k_pair = remote(k_in.at[:, other_lanes], kb.at[h], kv_send.at[0], kv_recv.at[0], partner)
    v_pair = remote(v_in.at[:, other_lanes], vb.at[h], kv_send.at[1], kv_recv.at[1], partner)
    sends = [q_pair, k_pair, v_pair]
    for copy in sends:
        copy.start()
    for side in range(2):

        @pl.when(has[side])
        def _():
            for copy in q_sends(side):
                copy.start()


    loads[2].wait()
    loads[3].wait()
    loads[4].wait()

    def grad_far(w, side):
        copies = []
        rows = rows_of(w)
        for n in range(2):
            slot = 2 + 2 * side + h
            where = {"tm": sides[side], "space": n}
            index = side * 2 + n
            copies.append(
                remote(stsend.at[n, w], st.at[slot, w], s_send.at[w, index], s_recv.at[slot, w], where)
            )
            copies.append(
                remote(
                    dsend.at[n, rows], db.at[slot, rows], d_send.at[w, index], d_recv.at[slot, w], where
                )
            )
        return copies

    def grad_pair(w):
        copies = []
        rows = rows_of(w)
        copies.append(
            remote(stsend.at[other, w], st.at[h, w], s_send.at[w, 4], s_recv.at[h, w], partner)
        )
        copies.append(
            remote(dsend.at[other, rows], db.at[h, rows], d_send.at[w, 4], d_recv.at[h, w], partner)
        )
        return copies

    def project(w, carry):
        rows = rows_of(w)
        pltpu.make_async_copy(cot_in.at[rows], cot_v.at[rows], lsem.at[8 + w]).wait()
        cot = cot_v[rows, :]
        down_grad = (adapter_factor * dot(cot, up_v[...], NT)).astype(bf16)
        dmix[rows, :] = down_grad
        grad = (dot(cot, w_v[...], NT) + dot(down_grad, down_v[...])).astype(bf16)
        product = (grad.astype(f32) * o_v[rows, :].astype(f32)).T
        for n in range(2):
            delta = jnp.sum(product[n * hd : (n + 1) * hd, :], axis=0, keepdims=True)
            stsend[n, w, 0:1, :] = lse_v[w, n : n + 1, :] * LOG2E
            stsend[n, w, 1:2, :] = delta
            dsend[n, rows, :] = grad[:, n * hd : (n + 1) * hd]
        db[h, rows, :] = dsend[h, rows, :]
        st[h, w] = stsend[h, w]
        return carry

    lax.fori_loop(0, 2, project, 0)

    ranks = pa.shape[1] // 2
    lanes = pb.shape[2]
    features = ga.shape[1]
    oct_sends = []
    for step in range(4):
        peer, where = quad(step)
        if step:
            oct_sends.append(
                remote(
                    pa.at[peer], ra.at[step - 1], oc_ssem.at[step - 1], oc_rsem.at[step - 1], where
                )
            )
        oct_sends.append(
            remote(
                pb.at[peer],
                rb.at[step],
                oc_ssem.at[3 + step],
                oc_rsem.at[3 + step],
                {**where, "tensor": 2 * y + 1 - x_hi},
            )
        )
    z_sends = []
    for step in range(1, z_size):
        z_sends.append(
            remote(
                zb.at[z],
                zb.at[z],
                z_ssem.at[step - 1],
                z_rsem.at[step - 1],
                {"tm": x_lo * z_size + lax.rem(z + step, z_size)},
            )
        )
    quad_sends = []
    for step in range(1, 4):
        quad_sends.append(
            remote(
                fq.at[quarter], fq.at[quarter], f_ssem.at[step - 1], f_rsem.at[step - 1], quad(step)[1]
            )
        )

    def adapter_parts():
        for copy in mx_sends:
            copy.wait_recv()
        mixed = mx_own[...].astype(f32)
        for index in range(y_size - 1):
            mixed += mx[index].astype(f32)
        mixed = mixed.astype(bf16)
        parts = []
        for side in range(2):
            columns = pl.ds(pl.multiple_of((2 * y + side) * cols, 128), cols)
            parts.append(dot(mixed, cot_v[:, columns]) * (adapter_factor / total_tokens))
        a_part = dot(dmix[...], o_v[...], TN) * (1.0 / total_tokens)
        first = x_hi == 0
        same = jnp.where(first, parts[0], parts[1])
        across = jnp.where(first, parts[1], parts[0])
        for p in range(4):
            rows = slice(p * ranks, (p + 1) * ranks)
            pa[p, :ranks, :cols] = same[rows, :].astype(bf16)
            pa[p, ranks:, :features] = a_part[rows, :].astype(bf16)
            pb[p, :ranks, :] = across[rows, :lanes].astype(bf16)
            pb[p, ranks:, : cols - lanes] = across[rows, lanes:].astype(bf16)
        for copy in oct_sends:
            copy.start()

    def adapter_z():
        for copy in oct_sends:
            copy.wait_recv()
        total = pa[quarter].astype(f32)
        for index in range(3):
            total += ra[index].astype(f32)
        other_up = rb[0].astype(f32)
        for index in range(1, 4):
            other_up += rb[index].astype(f32)
        up_total = total[:ranks, :cols] + jnp.concatenate(
            [other_up[:ranks, :], other_up[ranks:, : cols - lanes]], axis=1
        )
        zb[z, :ranks, :cols] = up_total.astype(bf16)
        zb[z, ranks:, :features] = total[ranks:, :features].astype(bf16)
        for copy in z_sends:
            copy.start()

    def adapter_quad():
        for copy in z_sends:
            copy.wait_recv()
        total = zb[0].astype(f32)
        for index in range(1, z_size):
            total += zb[index].astype(f32)
        fq[quarter] = total
        for copy in quad_sends:
            copy.start()

    def adapter_out():
        for copy in quad_sends:
            copy.wait_recv()
        for p in range(4):
            rows = slice(p * ranks, (p + 1) * ranks)
            um[rows, :] = fq[p, :ranks, :cols]
            ga[rows, :] = fq[p, ranks:, :features]

    zb[z] = jnp.zeros(zb.shape[1:], bf16)
    pa[...] = jnp.zeros_like(pa)
    pb[...] = jnp.zeros_like(pb)

    def start_far(w):
        for side in range(2):

            @pl.when(has[side])
            def _():
                for copy in grad_far(w, side):
                    copy.start()

    for copy in grad_pair(0) + grad_pair(1):
        copy.start()
    start_far(0)
    adapter_parts()
    start_far(1)

    for copy in loads[5:]:
        copy.wait()
    k_pair.wait_recv()
    v_pair.wait_recv()
    dk_acc[...] = jnp.zeros_like(dk_acc)
    dv_acc[...] = jnp.zeros_like(dv_acc)
    for row in range(2):
        kt_buf[:, row * 2 * tile : (row + 1) * 2 * tile] = kb[row].T

    for side in range(2):

        @pl.when(jnp.logical_not(has[1 - side]))
        def _():
            for slot in (2 + 2 * side, 3 + 2 * side):
                qb[slot] = jnp.zeros(qb.shape[1:], bf16)
                db[slot] = jnp.zeros(db.shape[1:], bf16)
                st[slot] = jnp.zeros(st.shape[1:], f32)
            ret[side] = jnp.zeros(ret.shape[1:], bf16)

    reach_t = reach[h, 0]
    reach_h = reach[h, 1]
    reach_w = reach[h, 2]

    def locate(u):
        v = u - 2
        near = u < 2
        w = jnp.where(near, u, v // 2)
        row = lax.rem(v + 2, 2)
        slots = (jnp.where(near, 0, 2 + row), jnp.where(near, 1, 4 + row))
        return near, w, row, slots

    def back(u, side):
        _, w, row, _ = locate(u)
        where = {"tm": (left, right)[side], "space": row}
        return remote(
            rq.at[u, side],
            ret.at[1 - side, h, rows_of(w)],
            r_send.at[u, side],
            r_recv.at[2 * (1 - side) + h, w],
            where,
        )

    def back_pair(u):
        rows = rows_of(u)
        return remote(
            rq.at[u, other], ret.at[2, h, rows], r_send.at[u, other], r_recv.at[4 + h, u], partner
        )

    def arrive(slot, w):
        rows = rows_of(w)
        remote(st.at[slot, w], st.at[slot, w], s_send.at[0, 0], s_recv.at[slot, w], partner).wait_recv()
        remote(
            db.at[slot, rows], db.at[slot, rows], d_send.at[0, 0], d_recv.at[slot, w], partner
        ).wait_recv()

        @pl.when(w == 0)
        def _():
            remote(qb.at[slot], qb.at[slot], q_send.at[0], q_recv.at[slot], partner).wait_recv()

    def step(u, carry):
        near, w, row, slots = locate(u)
        rows = rows_of(w)

        @pl.when(near)
        def _():
            arrive(other, w)

        @pl.when(u == 4)
        def _():
            adapter_z()

        @pl.when(u >= 2)
        def _():
            for side in range(2):

                @pl.when(has[1 - side])
                def _():
                    arrive(slots[side], w)

        q = jnp.concatenate([qb[slot, rows, :] for slot in slots], axis=0)
        d = jnp.concatenate([db[slot, rows, :] for slot in slots], axis=0)
        lse = [st[slot, w, 0:1, :] for slot in slots]
        delta = jnp.concatenate([st[slot, w, 1:2, :] for slot in slots], axis=1)
        frame_ok = [near | ((reach_t >= 1) & (t > 0)), near | ((reach_t >= 1) & (t < t_size - 1))]
        height = [jnp.where(near, 0, row), jnp.where(near, 1, row)]
        dq = None
        for kt in range(4):
            hk, wk = kt // 2, kt % 2
            key_ok = (jnp.abs(w - wk) <= reach_w) & (valid[hk, wk, t] == 1)
            shift = jnp.concatenate(
                [
                    lse[side]
                    + jnp.where(
                        key_ok & frame_ok[side] & (jnp.abs(height[side] - hk) <= reach_h), 0.0, FAR
                    )
                    for side in range(2)
                ],
                axis=1,
            )
            k = kb[hk, wk * tile : (wk + 1) * tile, :]
            v = vb[hk, wk * tile : (wk + 1) * tile, :]
            probs = jnp.exp2(dot(k, q, NT) * (scale * LOG2E) - shift)
            dprobs = dot(v, d, NT)
            dscore = (probs * (dprobs - delta)).astype(bf16)
            span = slice(kt * tile, (kt + 1) * tile)
            dv_acc[span, :] += dot(probs.astype(bf16), d)
            dk_acc[span, :] += dot(dscore, q)
            part = dot(kt_buf[:, span], dscore)
            dq = part if dq is None else dq + part
        dq_rows = (dq * scale).T.astype(bf16)
        for side in range(2):
            rq[u, side] = dq_rows[side * tile : (side + 1) * tile, :]

        for side in range(2):

            @pl.when((u >= 2) & has[1 - side])
            def _():
                back(u, side).start()

        @pl.when(near)
        def _():
            back_pair(u).start()
            ret[2, h, rows, :] = rq[u, h]

        return carry

    lax.fori_loop(0, 6, step, 0)

    for row in range(2):
        dkb[row] = (dk_acc[row * 2 * tile : (row + 1) * 2 * tile, :] * scale).astype(bf16)
        dvb[row] = dv_acc[row * 2 * tile : (row + 1) * 2 * tile, :].astype(bf16)
    pair_out = [
        remote(dkb.at[other], gk.at[:, mine_lanes], out_send.at[0], out_recv.at[0], partner),
        remote(dvb.at[other], gv.at[:, mine_lanes], out_send.at[1], out_recv.at[1], partner),
    ]
    own_out = [
        pltpu.make_async_copy(dkb.at[h], gk.at[:, mine_lanes], out_sem.at[0]),
        pltpu.make_async_copy(dvb.at[h], gv.at[:, mine_lanes], out_sem.at[1]),
    ]
    for copy in pair_out + own_out:
        copy.start()

    adapter_quad()

    for w in range(2):
        rows = rows_of(w)
        for side in range(2):

            @pl.when(has[1 - side])
            def _():
                for n in range(2):
                    remote(
                        ret.at[side, n, rows],
                        ret.at[side, n, rows],
                        r_send.at[0, 0],
                        r_recv.at[2 * side + n, w],
                        partner,
                    ).wait_recv()

        remote(
            ret.at[2, other, rows], ret.at[2, other, rows], r_send.at[0, 0], r_recv.at[4 + other, w], partner
        ).wait_recv()
        for n in range(2):
            total = (
                ret[0, n, rows, :].astype(f32)
                + ret[1, n, rows, :].astype(f32)
                + ret[2, n, rows, :].astype(f32)
            )
            gq_v[rows, n * hd : (n + 1) * hd] = total.astype(bf16)
    gq_copy = pltpu.make_async_copy(gq_v, gq, out_sem.at[2])
    gq_copy.start()

    adapter_out()

    for copy in sends + mx_sends + oct_sends + z_sends + quad_sends + pair_out:
        copy.wait_send()
    for w in range(2):
        for copy in grad_pair(w):
            copy.wait_send()
    for side in range(2):

        @pl.when(has[side])
        def _():
            for copy in q_sends(side):
                copy.wait_send()
            for w in range(2):
                for copy in grad_far(w, side):
                    copy.wait_send()


    def drain(u, carry):
        for side in range(2):

            @pl.when(has[1 - side])
            def _():
                back(u, side).wait_send()

        return carry

    lax.fori_loop(2, 6, drain, 0)
    for u in range(2):
        back_pair(u).wait_send()
    for copy in pair_out:
        copy.wait_recv()
    for copy in own_out + [gq_copy]:
        copy.wait()


def finish(*refs):
    count = len(refs) // 2
    for index in range(count):
        refs[count + index][...] = refs[index][...]


def body(
    queries,
    keys,
    values,
    attention_output,
    row_logsumexp,
    output_cotangent,
    output_weight,
    adapter_down,
    adapter_up,
    head_tile_reach,
    key_tile_valid,
):
    tile = queries.shape[3]
    features = queries.shape[4]
    tokens = queries.shape[2] * tile
    heads = head_tile_reach.shape[0]
    hd = features // heads
    rank = adapter_down.shape[1]
    model = output_cotangent.shape[4]
    t_size = lax.axis_size("tm")
    g_size = lax.axis_size("tensor")
    total_tokens = t_size * lax.axis_size("space") * tokens
    cols = model // g_size
    width = max(cols, features)
    ranks = rank // 4
    lanes = -(-cols // 256) * 128
    y_size = g_size // 2
    sizes = (tile, hd, t_size, g_size, total_tokens, cols)

    def flat(array):
        return array.reshape(tokens, array.shape[-1])

    anywhere = pl.BlockSpec(memory_space=pl.ANY)
    hbm = pl.BlockSpec(memory_space=pltpu.HBM)
    vmem = pl.BlockSpec(memory_space=pltpu.VMEM)
    smem = pl.BlockSpec(memory_space=pltpu.SMEM)
    dma = pltpu.SemaphoreType.DMA
    grads = jax.ShapeDtypeStruct((tokens, features), bf16)
    scratch = [
        pltpu.VMEM((6, tokens, hd), bf16),
        pltpu.VMEM((6, tokens, hd), bf16),
        pltpu.VMEM((6, 2, 8, tile), f32),
        pltpu.VMEM((2, tokens, hd), bf16),
        pltpu.VMEM((2, tokens, hd), bf16),
        pltpu.VMEM((hd, 2 * tokens), bf16),
        pltpu.VMEM((tokens, features), bf16),
        pltpu.VMEM((2, heads, tile), f32),
        pltpu.VMEM((tokens, model), bf16),
        pltpu.VMEM((features, model), bf16),
        pltpu.VMEM((rank, features), bf16),
        pltpu.VMEM((rank, model), bf16),
        pltpu.VMEM((2, tokens, hd), bf16),
        pltpu.VMEM((2, 2, 8, tile), f32),
        pltpu.VMEM((tokens, rank), bf16),
        pltpu.VMEM((2 * tokens, hd), f32),
        pltpu.VMEM((2 * tokens, hd), f32),
        pltpu.VMEM((6, 2, tile, hd), bf16),
        pltpu.VMEM((3, 2, tokens, hd), bf16),
        pltpu.VMEM((tokens, features), bf16),
        pltpu.VMEM((2, tokens, hd), bf16),
        pltpu.VMEM((2, tokens, hd), bf16),
        pltpu.VMEM((rank, tokens), bf16),
        pltpu.VMEM((max(y_size - 1, 1), rank, tokens), bf16),
        pltpu.VMEM((4, 2 * ranks, width), bf16),
        pltpu.VMEM((4, 2 * ranks, lanes), bf16),
        pltpu.VMEM((3, 2 * ranks, width), bf16),
        pltpu.VMEM((4, 2 * ranks, lanes), bf16),
        pltpu.VMEM((t_size // 2, 2 * ranks, width), bf16),
        pltpu.VMEM((4, 2 * ranks, width), f32),
        pltpu.SMEM(head_tile_reach.shape, jnp.int32),
        pltpu.SMEM(key_tile_valid.shape[1:] + key_tile_valid.shape[:1], jnp.int32),
        dma((12,)),
        dma((5,)),
        dma((6,)),
        dma((2, 5)),
        dma((6, 2)),
        dma((2, 5)),
        dma((6, 2)),
        dma((2,)),
        dma((2,)),
        dma((6, 2)),
        dma((6, 2)),
        dma((max(y_size - 1, 1),)),
        dma((max(y_size - 1, 1),)),
        dma((7,)),
        dma((7,)),
        dma((t_size // 2 - 1,)),
        dma((t_size // 2 - 1,)),
        dma((3,)),
        dma((3,)),
        dma((2,)),
        dma((2,)),
        dma((3,)),
    ]
    results = pl.pallas_call(
        functools.partial(kernel, sizes),
        out_shape=(
            grads,
            grads,
            grads,
            jax.ShapeDtypeStruct((rank, features), f32),
            jax.ShapeDtypeStruct((rank, cols), f32),
        ),
        in_specs=[hbm] * 11,
        out_specs=(anywhere, anywhere, anywhere, vmem, vmem),
        scratch_shapes=scratch,
        compiler_params=pltpu.CompilerParams(
            collective_id=0, has_side_effects=True, vmem_limit_bytes=62 * 1024 * 1024
        ),
    )(
        flat(queries),
        flat(keys),
        flat(values),
        flat(attention_output),
        row_logsumexp.reshape(row_logsumexp.shape[2:]),
        flat(output_cotangent),
        output_weight,
        adapter_down.T,
        adapter_up,
        head_tile_reach,
        jnp.transpose(key_tile_valid, (1, 2, 0)),
    )
    grad_q, grad_k, grad_v, grad_a, up_map_gradient = pl.pallas_call(
        finish,
        out_shape=tuple(jax.ShapeDtypeStruct(array.shape, array.dtype) for array in results),
        in_specs=[vmem] * 5,
        out_specs=(vmem,) * 5,
        compiler_params=pltpu.CompilerParams(vmem_limit_bytes=62 * 1024 * 1024),
    )(*results)
    return (
        grad_q.reshape(queries.shape),
        grad_k.reshape(queries.shape),
        grad_v.reshape(queries.shape),
        grad_a.T,
        up_map_gradient,
    )


def solution(mesh):
    placed = (
        P("tm", "space", None, None, "tensor"),
        P("tm", "space", None, None, "tensor"),
        P("tm", "space", None, None, "tensor"),
        P("tm", "space", None, None, "tensor"),
        P("tm", "space", None, "tensor", None),
        P("tm", "space", None, None, None),
        P("tensor", None),
        P("tensor", None),
        P(),
        P("tensor", None),
        P(),
    )
    return jax.shard_map(
        body,
        mesh=mesh,
        in_specs=placed,
        out_specs=(
            P("tm", "space", None, None, "tensor"),
            P("tm", "space", None, None, "tensor"),
            P("tm", "space", None, None, "tensor"),
            P("tensor", None),
            P(None, "tensor"),
        ),
        check_vma=False,
    )
```

```python
import functools

import jax
import jax.numpy as jnp
from jax import lax
from jax.experimental import pallas as pl
from jax.experimental.pallas import tpu as pltpu
from jax.sharding import PartitionSpec as P

adapter_factor = 2.0
LOG2E = 1.4426950408889634
FAR = 1e30
MESH = pl.DeviceIdType.MESH
NT = (((1,), (1,)), ((), ()))
TN = (((0,), (0,)), ((), ()))
f32 = jnp.float32
bf16 = jnp.bfloat16


def dot(a, b, dims=(((1,), (0,)), ((), ()))):
    return lax.dot_general(a, b, dims, preferred_element_type=f32)


def kernel(
    sizes,
    q_in,
    k_in,
    v_in,
    o_in,
    lse_in,
    cot_in,
    w_in,
    down_in,
    up_in,
    reach_in,
    valid_in,
    gq,
    gk,
    gv,
    fq,
    qb,
    db,
    st,
    kb,
    vb,
    kt_buf,
    o_v,
    lse_v,
    cot_v,
    w_v,
    down_v,
    up_v,
    dsend,
    stsend,
    dmix,
    dk_acc,
    dv_acc,
    rq,
    ret,
    gq_v,
    dkb,
    dvb,
    mx_own,
    mx,
    pa,
    pb,
    ra,
    rb,
    zb,
    f_own,
    reach,
    valid,
    lsem,
    q_send,
    q_recv,
    d_send,
    d_recv,
    s_send,
    s_recv,
    kv_send,
    kv_recv,
    r_send,
    r_recv,
    mx_ssem,
    mx_rsem,
    oc_ssem,
    oc_rsem,
    z_ssem,
    z_rsem,
    f_ssem,
    f_rsem,
    out_send,
    out_recv,
    out_sem,
):
    tile, hd, t_size, g_size, total_tokens, cols = sizes
    t = lax.axis_index("tm")
    h = lax.axis_index("space")
    g = lax.axis_index("tensor")
    other = 1 - h
    left = lax.rem(t + t_size - 1, t_size)
    right = lax.rem(t + 1, t_size)
    z_size = t_size // 2
    y_size = g_size // 2
    x_lo = t // z_size
    z = lax.rem(t, z_size)
    y = g // 2
    x_hi = lax.rem(g, 2)
    quarter = 2 * x_lo + h
    scale = hd**-0.5
    mine_lanes = pl.ds(pl.multiple_of(h * hd, hd), hd)
    other_lanes = pl.ds(pl.multiple_of(other * hd, hd), hd)

    def quad(step):
        peer = lax.rem(quarter + step, 4)
        return peer, {"tm": lax.rem(peer // 2, 2) * z_size + z, "space": lax.rem(peer, 2)}

    sides = (right, left)
    partner = {"space": other}
    has = (t < t_size - 1, t > 0)

    def local(src, dst, index):
        return pltpu.make_async_copy(src, dst, lsem.at[index])

    def remote(src, dst, ssem, rsem, where):
        return pltpu.make_async_remote_copy(
            src_ref=src, dst_ref=dst, send_sem=ssem, recv_sem=rsem, device_id=where, device_id_type=MESH
        )

    def rows_of(w):
        return pl.ds(pl.multiple_of(w * tile, tile), tile)

    loads = [
        local(o_in, o_v, 0),
        local(down_in, down_v, 1),
        local(w_in, w_v, 2),
        local(up_in, up_v, 3),
        local(lse_in, lse_v, 4),
        local(q_in.at[:, mine_lanes], qb.at[h], 5),
        local(k_in.at[:, mine_lanes], kb.at[h], 6),
        local(v_in.at[:, mine_lanes], vb.at[h], 7),
        local(reach_in, reach, 10),
        local(valid_in, valid, 11),
    ]
    for copy in loads[:4]:
        copy.start()
    cot_loads = [local(cot_in.at[rows_of(w)], cot_v.at[rows_of(w)], 8 + w) for w in range(2)]
    for copy in cot_loads + loads[4:]:
        copy.start()

    barrier = pltpu.get_barrier_semaphore()
    greeted = [{"tm": side, "space": n} for side in (left, right) for n in range(2)]
    greeted += [{"tensor": lax.rem(y + step, y_size) * 2 + x_hi} for step in range(1, y_size)]
    greeted += [quad(step)[1] for step in range(1, 4)]
    greeted += [{**quad(step)[1], "tensor": 2 * y + 1 - x_hi} for step in range(4)]
    greeted += [{"tm": x_lo * z_size + lax.rem(z + step, z_size)} for step in range(1, z_size)]
    for where in greeted:
        pl.semaphore_signal(barrier, inc=1, device_id=where, device_id_type=MESH)
    loads[0].wait()
    loads[1].wait()
    mixed_part = dot(down_v[...], o_v[...], NT)
    mx_own[...] = mixed_part.astype(bf16)

    pl.semaphore_wait(barrier, len(greeted))

    mx_sends = []
    for step in range(1, y_size):
        mx_sends.append(
            remote(
                mx_own,
                mx.at[step - 1],
                mx_ssem.at[step - 1],
                mx_rsem.at[step - 1],
                {"tensor": lax.rem(y + step, y_size) * 2 + x_hi},
            )
        )
    for copy in mx_sends:
        copy.start()

    def q_sends(side):
        return [
            remote(
                q_in.at[:, n * hd : (n + 1) * hd],
                qb.at[2 + 2 * side + h],
                q_send.at[side * 2 + n],
                q_recv.at[2 + 2 * side + h],
                {"tm": sides[side], "space": n},
            )
            for n in range(2)
        ]

    q_pair = remote(q_in.at[:, other_lanes], qb.at[h], q_send.at[4], q_recv.at[h], partner)
    k_pair = remote(k_in.at[:, other_lanes], kb.at[h], kv_send.at[0], kv_recv.at[0], partner)
    v_pair = remote(v_in.at[:, other_lanes], vb.at[h], kv_send.at[1], kv_recv.at[1], partner)
    sends = [q_pair, k_pair, v_pair]
    for copy in sends:
        copy.start()
    for side in range(2):

        @pl.when(has[side])
        def _():
            for copy in q_sends(side):
                copy.start()


    loads[2].wait()
    loads[3].wait()
    loads[4].wait()

    def grad_far(w, side):
        copies = []
        rows = rows_of(w)
        for n in range(2):
            slot = 2 + 2 * side + h
            where = {"tm": sides[side], "space": n}
            index = side * 2 + n
            copies.append(
                remote(stsend.at[n, w], st.at[slot, w], s_send.at[w, index], s_recv.at[slot, w], where)
            )
            copies.append(
                remote(
                    dsend.at[n, rows], db.at[slot, rows], d_send.at[w, index], d_recv.at[slot, w], where
                )
            )
        return copies

    def grad_pair(w):
        copies = []
        rows = rows_of(w)
        copies.append(
            remote(stsend.at[other, w], st.at[h, w], s_send.at[w, 4], s_recv.at[h, w], partner)
        )
        copies.append(
            remote(dsend.at[other, rows], db.at[h, rows], d_send.at[w, 4], d_recv.at[h, w], partner)
        )
        return copies

    def project(w, carry):
        rows = rows_of(w)
        pltpu.make_async_copy(cot_in.at[rows], cot_v.at[rows], lsem.at[8 + w]).wait()
        cot = cot_v[rows, :]
        down_grad = (adapter_factor * dot(cot, up_v[...], NT)).astype(bf16)
        dmix[rows, :] = down_grad
        grad = (dot(cot, w_v[...], NT) + dot(down_grad, down_v[...])).astype(bf16)
        product = (grad.astype(f32) * o_v[rows, :].astype(f32)).T
        for n in range(2):
            delta = jnp.sum(product[n * hd : (n + 1) * hd, :], axis=0, keepdims=True)
            stsend[n, w, 0:1, :] = lse_v[w, n : n + 1, :] * LOG2E
            stsend[n, w, 1:2, :] = delta
            dsend[n, rows, :] = grad[:, n * hd : (n + 1) * hd]
        db[h, rows, :] = dsend[h, rows, :]
        st[h, w] = stsend[h, w]
        return carry

    lax.fori_loop(0, 2, project, 0)

    ranks = pa.shape[1] // 2
    lanes = pb.shape[2]
    features = o_v.shape[1]
    oct_sends = []
    for step in range(4):
        peer, where = quad(step)
        if step:
            oct_sends.append(
                remote(
                    pa.at[peer], ra.at[step - 1], oc_ssem.at[step - 1], oc_rsem.at[step - 1], where
                )
            )
        oct_sends.append(
            remote(
                pb.at[peer],
                rb.at[step],
                oc_ssem.at[3 + step],
                oc_rsem.at[3 + step],
                {**where, "tensor": 2 * y + 1 - x_hi},
            )
        )
    z_sends = []
    for step in range(1, z_size):
        z_sends.append(
            remote(
                zb.at[z],
                zb.at[z],
                z_ssem.at[step - 1],
                z_rsem.at[step - 1],
                {"tm": x_lo * z_size + lax.rem(z + step, z_size)},
            )
        )
    quad_sends = []
    for step in range(1, 4):
        quad_sends.append(
            remote(
                f_own, fq.at[quarter], f_ssem.at[step - 1], f_rsem.at[step - 1], quad(step)[1]
            )
        )

    f_copy = pltpu.make_async_copy(f_own, fq.at[quarter], out_sem.at[3])

    def adapter_parts():
        for copy in mx_sends:
            copy.wait_recv()
        mixed = mx_own[...].astype(f32)
        for index in range(y_size - 1):
            mixed += mx[index].astype(f32)
        mixed = mixed.astype(bf16)
        parts = []
        for side in range(2):
            columns = pl.ds(pl.multiple_of((2 * y + side) * cols, 128), cols)
            parts.append(dot(mixed, cot_v[:, columns]) * (adapter_factor / total_tokens))
        a_part = dot(dmix[...], o_v[...], TN) * (1.0 / total_tokens)
        first = x_hi == 0
        same = jnp.where(first, parts[0], parts[1])
        across = jnp.where(first, parts[1], parts[0])
        for p in range(4):
            rows = slice(p * ranks, (p + 1) * ranks)
            pa[p, :ranks, :cols] = same[rows, :].astype(bf16)
            pa[p, ranks:, :features] = a_part[rows, :].astype(bf16)
            pb[p, :ranks, :] = across[rows, :lanes].astype(bf16)
            pb[p, ranks:, : cols - lanes] = across[rows, lanes:].astype(bf16)
        for copy in oct_sends:
            copy.start()

    def adapter_z():
        for copy in oct_sends:
            copy.wait_recv()
        total = pa[quarter].astype(f32)
        for index in range(3):
            total += ra[index].astype(f32)
        other_up = rb[0].astype(f32)
        for index in range(1, 4):
            other_up += rb[index].astype(f32)
        up_total = total[:ranks, :cols] + jnp.concatenate(
            [other_up[:ranks, :], other_up[ranks:, : cols - lanes]], axis=1
        )
        zb[z, :ranks, :cols] = up_total.astype(bf16)
        zb[z, ranks:, :features] = total[ranks:, :features].astype(bf16)
        for copy in z_sends:
            copy.start()

    def adapter_quad():
        for copy in z_sends:
            copy.wait_recv()
        total = zb[0].astype(f32)
        for index in range(1, z_size):
            total += zb[index].astype(f32)
        f_own[...] = total.astype(bf16)
        for copy in quad_sends + [f_copy]:
            copy.start()

    zb[z] = jnp.zeros(zb.shape[1:], bf16)
    pa[...] = jnp.zeros_like(pa)
    pb[...] = jnp.zeros_like(pb)

    def start_far(w):
        for side in range(2):

            @pl.when(has[side])
            def _():
                for copy in grad_far(w, side):
                    copy.start()

    for copy in grad_pair(0) + grad_pair(1):
        copy.start()
    start_far(0)
    adapter_parts()
    start_far(1)

    for copy in loads[5:]:
        copy.wait()
    k_pair.wait_recv()
    v_pair.wait_recv()
    dk_acc[...] = jnp.zeros_like(dk_acc)
    dv_acc[...] = jnp.zeros_like(dv_acc)
    for row in range(2):
        kt_buf[:, row * 2 * tile : (row + 1) * 2 * tile] = kb[row].T

    for side in range(2):

        @pl.when(jnp.logical_not(has[1 - side]))
        def _():
            for slot in (2 + 2 * side, 3 + 2 * side):
                qb[slot] = jnp.zeros(qb.shape[1:], bf16)
                db[slot] = jnp.zeros(db.shape[1:], bf16)
                st[slot] = jnp.zeros(st.shape[1:], f32)
            ret[side] = jnp.zeros(ret.shape[1:], bf16)

    reach_t = reach[h, 0]
    reach_h = reach[h, 1]
    reach_w = reach[h, 2]

    def locate(u):
        v = u - 2
        near = u < 2
        w = jnp.where(near, u, v // 2)
        row = lax.rem(v + 2, 2)
        slots = (jnp.where(near, 0, 2 + row), jnp.where(near, 1, 4 + row))
        return near, w, row, slots

    def back(u, side):
        _, w, row, _ = locate(u)
        where = {"tm": (left, right)[side], "space": row}
        return remote(
            rq.at[u, side],
            ret.at[1 - side, h, rows_of(w)],
            r_send.at[u, side],
            r_recv.at[2 * (1 - side) + h, w],
            where,
        )

    def back_pair(u):
        rows = rows_of(u)
        return remote(
            rq.at[u, other], ret.at[2, h, rows], r_send.at[u, other], r_recv.at[4 + h, u], partner
        )

    def arrive(slot, w):
        rows = rows_of(w)
        remote(st.at[slot, w], st.at[slot, w], s_send.at[0, 0], s_recv.at[slot, w], partner).wait_recv()
        remote(
            db.at[slot, rows], db.at[slot, rows], d_send.at[0, 0], d_recv.at[slot, w], partner
        ).wait_recv()

        @pl.when(w == 0)
        def _():
            remote(qb.at[slot], qb.at[slot], q_send.at[0], q_recv.at[slot], partner).wait_recv()

    def step(u, carry):
        near, w, row, slots = locate(u)
        rows = rows_of(w)

        @pl.when(near)
        def _():
            arrive(other, w)

        @pl.when(u == 4)
        def _():
            adapter_z()

        @pl.when(u >= 2)
        def _():
            for side in range(2):

                @pl.when(has[1 - side])
                def _():
                    arrive(slots[side], w)

        q = jnp.concatenate([qb[slot, rows, :] for slot in slots], axis=0)
        d = jnp.concatenate([db[slot, rows, :] for slot in slots], axis=0)
        lse = [st[slot, w, 0:1, :] for slot in slots]
        delta = jnp.concatenate([st[slot, w, 1:2, :] for slot in slots], axis=1)
        frame_ok = [near | ((reach_t >= 1) & (t > 0)), near | ((reach_t >= 1) & (t < t_size - 1))]
        height = [jnp.where(near, 0, row), jnp.where(near, 1, row)]
        dq = None
        for kt in range(4):
            hk, wk = kt // 2, kt % 2
            key_ok = (jnp.abs(w - wk) <= reach_w) & (valid[hk, wk, t] == 1)
            shift = jnp.concatenate(
                [
                    lse[side]
                    + jnp.where(
                        key_ok & frame_ok[side] & (jnp.abs(height[side] - hk) <= reach_h), 0.0, FAR
                    )
                    for side in range(2)
                ],
                axis=1,
            )
            k = kb[hk, wk * tile : (wk + 1) * tile, :]
            v = vb[hk, wk * tile : (wk + 1) * tile, :]
            probs = jnp.exp2(dot(k, q, NT) * (scale * LOG2E) - shift)
            dprobs = dot(v, d, NT)
            dscore = (probs * (dprobs - delta)).astype(bf16)
            span = slice(kt * tile, (kt + 1) * tile)
            dv_acc[span, :] += dot(probs.astype(bf16), d)
            dk_acc[span, :] += dot(dscore, q)
            part = dot(kt_buf[:, span], dscore)
            dq = part if dq is None else dq + part
        dq_rows = (dq * scale).T.astype(bf16)
        for side in range(2):
            rq[u, side] = dq_rows[side * tile : (side + 1) * tile, :]

        for side in range(2):

            @pl.when((u >= 2) & has[1 - side])
            def _():
                back(u, side).start()

        @pl.when(near)
        def _():
            back_pair(u).start()
            ret[2, h, rows, :] = rq[u, h]

        return carry

    lax.fori_loop(0, 6, step, 0)

    for row in range(2):
        dkb[row] = (dk_acc[row * 2 * tile : (row + 1) * 2 * tile, :] * scale).astype(bf16)
        dvb[row] = dv_acc[row * 2 * tile : (row + 1) * 2 * tile, :].astype(bf16)
    pair_out = [
        remote(dkb.at[other], gk.at[:, mine_lanes], out_send.at[0], out_recv.at[0], partner),
        remote(dvb.at[other], gv.at[:, mine_lanes], out_send.at[1], out_recv.at[1], partner),
    ]
    own_out = [
        pltpu.make_async_copy(dkb.at[h], gk.at[:, mine_lanes], out_sem.at[0]),
        pltpu.make_async_copy(dvb.at[h], gv.at[:, mine_lanes], out_sem.at[1]),
    ]
    for copy in pair_out + own_out:
        copy.start()

    adapter_quad()

    for w in range(2):
        rows = rows_of(w)
        for side in range(2):

            @pl.when(has[1 - side])
            def _():
                for n in range(2):
                    remote(
                        ret.at[side, n, rows],
                        ret.at[side, n, rows],
                        r_send.at[0, 0],
                        r_recv.at[2 * side + n, w],
                        partner,
                    ).wait_recv()

        remote(
            ret.at[2, other, rows], ret.at[2, other, rows], r_send.at[0, 0], r_recv.at[4 + other, w], partner
        ).wait_recv()
        for n in range(2):
            total = (
                ret[0, n, rows, :].astype(f32)
                + ret[1, n, rows, :].astype(f32)
                + ret[2, n, rows, :].astype(f32)
            )
            gq_v[rows, n * hd : (n + 1) * hd] = total.astype(bf16)
    gq_copy = pltpu.make_async_copy(gq_v, gq, out_sem.at[2])
    gq_copy.start()

    for copy in quad_sends:
        copy.wait_recv()

    for copy in sends + mx_sends + oct_sends + z_sends + quad_sends + pair_out:
        copy.wait_send()
    for w in range(2):
        for copy in grad_pair(w):
            copy.wait_send()
    for side in range(2):

        @pl.when(has[side])
        def _():
            for copy in q_sends(side):
                copy.wait_send()
            for w in range(2):
                for copy in grad_far(w, side):
                    copy.wait_send()


    def drain(u, carry):
        for side in range(2):

            @pl.when(has[1 - side])
            def _():
                back(u, side).wait_send()

        return carry

    lax.fori_loop(2, 6, drain, 0)
    for u in range(2):
        back_pair(u).wait_send()
    for copy in pair_out:
        copy.wait_recv()
    for copy in own_out + [gq_copy, f_copy]:
        copy.wait()


def finish(gq_in, gk_in, gv_in, fq_in, gq, gk, gv, ga, um, gq_v, gk_v, gv_v, fq_v, ga_v, um_v, sems):
    pairs = ((fq_in, fq_v), (gq_in, gq_v), (gk_in, gk_v), (gv_in, gv_v))
    reads = [pltpu.make_async_copy(*pair, sems.at[0, i]) for i, pair in enumerate(pairs)]
    pairs = ((ga_v, ga), (gq_v, gq), (gk_v, gk), (gv_v, gv), (um_v, um))
    writes = [pltpu.make_async_copy(*pair, sems.at[1, i]) for i, pair in enumerate(pairs)]
    for copy in reads:
        copy.start()
    for i in range(1, 4):
        reads[i].wait()
        writes[i].start()
    reads[0].wait()
    ranks = fq_v.shape[1] // 2
    for p in range(4):
        rows = slice(p * ranks, (p + 1) * ranks)
        um_v[rows, :] = fq_v[p, :ranks, : um_v.shape[1]].astype(f32)
        ga_v[rows, :] = fq_v[p, ranks:, : ga_v.shape[1]].astype(f32)
    writes[0].start()
    writes[4].start()
    for copy in writes:
        copy.wait()


def body(
    queries,
    keys,
    values,
    attention_output,
    row_logsumexp,
    output_cotangent,
    output_weight,
    adapter_down,
    adapter_up,
    head_tile_reach,
    key_tile_valid,
):
    tile = queries.shape[3]
    features = queries.shape[4]
    tokens = queries.shape[2] * tile
    heads = head_tile_reach.shape[0]
    hd = features // heads
    rank = adapter_down.shape[1]
    model = output_cotangent.shape[4]
    t_size = lax.axis_size("tm")
    g_size = lax.axis_size("tensor")
    total_tokens = t_size * lax.axis_size("space") * tokens
    cols = model // g_size
    width = max(cols, features)
    ranks = rank // 4
    lanes = -(-cols // 256) * 128
    y_size = g_size // 2
    sizes = (tile, hd, t_size, g_size, total_tokens, cols)

    def flat(array):
        return array.reshape(tokens, array.shape[-1])

    anywhere = pl.BlockSpec(memory_space=pl.ANY)
    hbm = pl.BlockSpec(memory_space=pltpu.HBM)
    dma = pltpu.SemaphoreType.DMA
    grads = jax.ShapeDtypeStruct((tokens, features), bf16)
    scratch = [
        pltpu.VMEM((6, tokens, hd), bf16),
        pltpu.VMEM((6, tokens, hd), bf16),
        pltpu.VMEM((6, 2, 8, tile), f32),
        pltpu.VMEM((2, tokens, hd), bf16),
        pltpu.VMEM((2, tokens, hd), bf16),
        pltpu.VMEM((hd, 2 * tokens), bf16),
        pltpu.VMEM((tokens, features), bf16),
        pltpu.VMEM((2, heads, tile), f32),
        pltpu.VMEM((tokens, model), bf16),
        pltpu.VMEM((features, model), bf16),
        pltpu.VMEM((rank, features), bf16),
        pltpu.VMEM((rank, model), bf16),
        pltpu.VMEM((2, tokens, hd), bf16),
        pltpu.VMEM((2, 2, 8, tile), f32),
        pltpu.VMEM((tokens, rank), bf16),
        pltpu.VMEM((2 * tokens, hd), f32),
        pltpu.VMEM((2 * tokens, hd), f32),
        pltpu.VMEM((6, 2, tile, hd), bf16),
        pltpu.VMEM((3, 2, tokens, hd), bf16),
        pltpu.VMEM((tokens, features), bf16),
        pltpu.VMEM((2, tokens, hd), bf16),
        pltpu.VMEM((2, tokens, hd), bf16),
        pltpu.VMEM((rank, tokens), bf16),
        pltpu.VMEM((max(y_size - 1, 1), rank, tokens), bf16),
        pltpu.VMEM((4, 2 * ranks, width), bf16),
        pltpu.VMEM((4, 2 * ranks, lanes), bf16),
        pltpu.VMEM((3, 2 * ranks, width), bf16),
        pltpu.VMEM((4, 2 * ranks, lanes), bf16),
        pltpu.VMEM((t_size // 2, 2 * ranks, width), bf16),
        pltpu.VMEM((2 * ranks, width), bf16),
        pltpu.SMEM(head_tile_reach.shape, jnp.int32),
        pltpu.SMEM(key_tile_valid.shape[1:] + key_tile_valid.shape[:1], jnp.int32),
        dma((12,)),
        dma((5,)),
        dma((6,)),
        dma((2, 5)),
        dma((6, 2)),
        dma((2, 5)),
        dma((6, 2)),
        dma((2,)),
        dma((2,)),
        dma((6, 2)),
        dma((6, 2)),
        dma((max(y_size - 1, 1),)),
        dma((max(y_size - 1, 1),)),
        dma((7,)),
        dma((7,)),
        dma((t_size // 2 - 1,)),
        dma((t_size // 2 - 1,)),
        dma((3,)),
        dma((3,)),
        dma((2,)),
        dma((2,)),
        dma((4,)),
    ]
    results = pl.pallas_call(
        functools.partial(kernel, sizes),
        out_shape=(
            grads,
            grads,
            grads,
            jax.ShapeDtypeStruct((4, 2 * ranks, width), bf16),
        ),
        in_specs=[hbm] * 11,
        out_specs=(anywhere,) * 4,
        scratch_shapes=scratch,
        compiler_params=pltpu.CompilerParams(
            collective_id=0, has_side_effects=True, vmem_limit_bytes=62 * 1024 * 1024
        ),
    )(
        flat(queries),
        flat(keys),
        flat(values),
        flat(attention_output),
        row_logsumexp.reshape(row_logsumexp.shape[2:]),
        flat(output_cotangent),
        output_weight,
        adapter_down.T,
        adapter_up,
        head_tile_reach,
        jnp.transpose(key_tile_valid, (1, 2, 0)),
    )
    totals = (jax.ShapeDtypeStruct((rank, features), f32), jax.ShapeDtypeStruct((rank, cols), f32))
    grad_q, grad_k, grad_v, grad_a, up_map_gradient = pl.pallas_call(
        finish,
        out_shape=(grads, grads, grads, *totals),
        in_specs=[anywhere] * 4,
        out_specs=(anywhere,) * 5,
        scratch_shapes=[pltpu.VMEM(array.shape, array.dtype) for array in (*results, *totals)]
        + [dma((2, 5))],
        compiler_params=pltpu.CompilerParams(vmem_limit_bytes=62 * 1024 * 1024),
    )(*results)
    return (
        grad_q.reshape(queries.shape),
        grad_k.reshape(queries.shape),
        grad_v.reshape(queries.shape),
        grad_a.T,
        up_map_gradient,
    )


def solution(mesh):
    placed = (
        P("tm", "space", None, None, "tensor"),
        P("tm", "space", None, None, "tensor"),
        P("tm", "space", None, None, "tensor"),
        P("tm", "space", None, None, "tensor"),
        P("tm", "space", None, "tensor", None),
        P("tm", "space", None, None, None),
        P("tensor", None),
        P("tensor", None),
        P(),
        P("tensor", None),
        P(),
    )
    return jax.shard_map(
        body,
        mesh=mesh,
        in_specs=placed,
        out_specs=(
            P("tm", "space", None, None, "tensor"),
            P("tm", "space", None, None, "tensor"),
            P("tm", "space", None, None, "tensor"),
            P("tensor", None),
            P(None, "tensor"),
        ),
        check_vma=False,
    )
```

```python
import functools

import jax
import jax.numpy as jnp
from jax import lax
from jax.experimental import pallas as pl
from jax.experimental.pallas import tpu as pltpu
from jax.sharding import PartitionSpec as P

adapter_factor = 2.0
LOG2E = 1.4426950408889634
FAR = 1e30
MESH = pl.DeviceIdType.MESH
NT = (((1,), (1,)), ((), ()))
TN = (((0,), (0,)), ((), ()))
f32 = jnp.float32
bf16 = jnp.bfloat16


def dot(a, b, dims=(((1,), (0,)), ((), ()))):
    return lax.dot_general(a, b, dims, preferred_element_type=f32)


def kernel(
    sizes,
    q_in,
    k_in,
    v_in,
    o_in,
    lse_in,
    cot_in,
    w_in,
    down_in,
    up_in,
    reach_in,
    valid_in,
    gq,
    gk,
    gv,
    fq,
    qb,
    db,
    st,
    kb,
    vb,
    kt_buf,
    o_v,
    lse_v,
    cot_v,
    w_v,
    down_v,
    up_v,
    dsend,
    stsend,
    dmix,
    dk_acc,
    dv_acc,
    rq,
    ret,
    gq_v,
    dkb,
    dvb,
    mx_own,
    mx,
    pa,
    pb,
    ra,
    rb,
    zb,
    f_own,
    reach,
    valid,
    lsem,
    q_send,
    q_recv,
    d_send,
    d_recv,
    s_send,
    s_recv,
    kv_send,
    kv_recv,
    r_send,
    r_recv,
    mx_ssem,
    mx_rsem,
    oc_ssem,
    oc_rsem,
    z_ssem,
    z_rsem,
    f_ssem,
    f_rsem,
    out_send,
    out_recv,
    out_sem,
):
    tile, hd, t_size, g_size, total_tokens, cols = sizes
    t = lax.axis_index("tm")
    h = lax.axis_index("space")
    g = lax.axis_index("tensor")
    other = 1 - h
    left = lax.rem(t + t_size - 1, t_size)
    right = lax.rem(t + 1, t_size)
    z_size = t_size // 2
    y_size = g_size // 2
    x_lo = t // z_size
    z = lax.rem(t, z_size)
    y = g // 2
    x_hi = lax.rem(g, 2)
    quarter = 2 * x_lo + h
    scale = hd**-0.5
    mine_lanes = pl.ds(pl.multiple_of(h * hd, hd), hd)
    other_lanes = pl.ds(pl.multiple_of(other * hd, hd), hd)

    def quad(step):
        peer = lax.rem(quarter + step, 4)
        return peer, {"tm": lax.rem(peer // 2, 2) * z_size + z, "space": lax.rem(peer, 2)}

    sides = (right, left)
    partner = {"space": other}
    has = (t < t_size - 1, t > 0)

    def local(src, dst, index):
        return pltpu.make_async_copy(src, dst, lsem.at[index])

    def remote(src, dst, ssem, rsem, where):
        return pltpu.make_async_remote_copy(
            src_ref=src, dst_ref=dst, send_sem=ssem, recv_sem=rsem, device_id=where, device_id_type=MESH
        )

    def rows_of(w):
        return pl.ds(pl.multiple_of(w * tile, tile), tile)

    loads = [
        local(o_in, o_v, 0),
        local(down_in, down_v, 1),
        local(w_in, w_v, 2),
        local(up_in, up_v, 3),
        local(lse_in, lse_v, 4),
        local(q_in.at[:, mine_lanes], qb.at[h], 5),
        local(k_in.at[:, mine_lanes], kb.at[h], 6),
        local(v_in.at[:, mine_lanes], vb.at[h], 7),
        local(reach_in, reach, 10),
        local(valid_in, valid, 11),
    ]
    for copy in loads[:4]:
        copy.start()
    cot_loads = [local(cot_in.at[rows_of(w)], cot_v.at[rows_of(w)], 8 + w) for w in range(2)]
    for copy in cot_loads + loads[4:]:
        copy.start()

    barrier = pltpu.get_barrier_semaphore()
    greeted = [{"tm": side, "space": n} for side in (left, right) for n in range(2)]
    greeted += [{"tensor": lax.rem(y + step, y_size) * 2 + x_hi} for step in range(1, y_size)]
    greeted += [quad(step)[1] for step in range(1, 4)]
    greeted += [{**quad(step)[1], "tensor": 2 * y + 1 - x_hi} for step in range(4)]
    greeted += [{"tm": x_lo * z_size + lax.rem(z + step, z_size)} for step in range(1, z_size)]
    for where in greeted:
        pl.semaphore_signal(barrier, inc=1, device_id=where, device_id_type=MESH)
    loads[0].wait()
    loads[1].wait()
    mixed_part = dot(down_v[...], o_v[...], NT)
    mx_own[...] = mixed_part.astype(bf16)

    pl.semaphore_wait(barrier, len(greeted))

    mx_sends = []
    for step in range(1, y_size):
        mx_sends.append(
            remote(
                mx_own,
                mx.at[step - 1],
                mx_ssem.at[step - 1],
                mx_rsem.at[step - 1],
                {"tensor": lax.rem(y + step, y_size) * 2 + x_hi},
            )
        )
    for copy in mx_sends:
        copy.start()

    def q_sends(side):
        return [
            remote(
                q_in.at[:, n * hd : (n + 1) * hd],
                qb.at[2 + 2 * side + h],
                q_send.at[side * 2 + n],
                q_recv.at[2 + 2 * side + h],
                {"tm": sides[side], "space": n},
            )
            for n in range(2)
        ]

    q_pair = remote(q_in.at[:, other_lanes], qb.at[h], q_send.at[4], q_recv.at[h], partner)
    k_pair = remote(k_in.at[:, other_lanes], kb.at[h], kv_send.at[0], kv_recv.at[0], partner)
    v_pair = remote(v_in.at[:, other_lanes], vb.at[h], kv_send.at[1], kv_recv.at[1], partner)
    sends = [q_pair, k_pair, v_pair]
    for copy in sends:
        copy.start()
    for side in range(2):

        @pl.when(has[side])
        def _():
            for copy in q_sends(side):
                copy.start()


    loads[2].wait()
    loads[3].wait()
    loads[4].wait()

    def grad_far(w, side):
        copies = []
        rows = rows_of(w)
        for n in range(2):
            slot = 2 + 2 * side + h
            where = {"tm": sides[side], "space": n}
            index = side * 2 + n
            copies.append(
                remote(stsend.at[n, w], st.at[slot, w], s_send.at[w, index], s_recv.at[slot, w], where)
            )
            copies.append(
                remote(
                    dsend.at[n, rows], db.at[slot, rows], d_send.at[w, index], d_recv.at[slot, w], where
                )
            )
        return copies

    def grad_pair(w):
        copies = []
        rows = rows_of(w)
        copies.append(
            remote(stsend.at[other, w], st.at[h, w], s_send.at[w, 4], s_recv.at[h, w], partner)
        )
        copies.append(
            remote(dsend.at[other, rows], db.at[h, rows], d_send.at[w, 4], d_recv.at[h, w], partner)
        )
        return copies

    def project(w, carry):
        rows = rows_of(w)
        pltpu.make_async_copy(cot_in.at[rows], cot_v.at[rows], lsem.at[8 + w]).wait()
        cot = cot_v[rows, :]
        down_grad = (adapter_factor * dot(cot, up_v[...], NT)).astype(bf16)
        dmix[rows, :] = down_grad
        grad = (dot(cot, w_v[...], NT) + dot(down_grad, down_v[...])).astype(bf16)
        product = (grad.astype(f32) * o_v[rows, :].astype(f32)).T
        for n in range(2):
            delta = jnp.sum(product[n * hd : (n + 1) * hd, :], axis=0, keepdims=True)
            stsend[n, w, 0:1, :] = lse_v[w, n : n + 1, :] * LOG2E
            stsend[n, w, 1:2, :] = delta
            dsend[n, rows, :] = grad[:, n * hd : (n + 1) * hd]
        db[h, rows, :] = dsend[h, rows, :]
        st[h, w] = stsend[h, w]
        return carry

    lax.fori_loop(0, 2, project, 0)

    ranks = pa.shape[1] // 2
    lanes = pb.shape[2]
    features = o_v.shape[1]
    oct_sends = []
    for step in range(4):
        peer, where = quad(step)
        if step:
            oct_sends.append(
                remote(
                    pa.at[peer], ra.at[step - 1], oc_ssem.at[step - 1], oc_rsem.at[step - 1], where
                )
            )
        oct_sends.append(
            remote(
                pb.at[peer],
                rb.at[step],
                oc_ssem.at[3 + step],
                oc_rsem.at[3 + step],
                {**where, "tensor": 2 * y + 1 - x_hi},
            )
        )
    z_sends = []
    for step in range(1, z_size):
        z_sends.append(
            remote(
                zb.at[z],
                zb.at[z],
                z_ssem.at[step - 1],
                z_rsem.at[step - 1],
                {"tm": x_lo * z_size + lax.rem(z + step, z_size)},
            )
        )
    quad_sends = []
    for step in range(1, 4):
        quad_sends.append(
            remote(
                f_own, fq.at[quarter], f_ssem.at[step - 1], f_rsem.at[step - 1], quad(step)[1]
            )
        )

    f_copy = pltpu.make_async_copy(f_own, fq.at[quarter], out_sem.at[3])

    def adapter_parts():
        for copy in mx_sends:
            copy.wait_recv()
        mixed = mx_own[...].astype(f32)
        for index in range(y_size - 1):
            mixed += mx[index].astype(f32)
        mixed = mixed.astype(bf16)
        parts = []
        for side in range(2):
            columns = pl.ds(pl.multiple_of((2 * y + side) * cols, 128), cols)
            parts.append(dot(mixed, cot_v[:, columns]) * (adapter_factor / total_tokens))
        a_part = dot(dmix[...], o_v[...], TN) * (1.0 / total_tokens)
        first = x_hi == 0
        same = jnp.where(first, parts[0], parts[1])
        across = jnp.where(first, parts[1], parts[0])
        for p in range(4):
            rows = slice(p * ranks, (p + 1) * ranks)
            pa[p, :ranks, :cols] = same[rows, :].astype(bf16)
            pa[p, ranks:, :features] = a_part[rows, :].astype(bf16)
            pb[p, :ranks, :] = across[rows, :lanes].astype(bf16)
            pb[p, ranks:, : cols - lanes] = across[rows, lanes:].astype(bf16)
        for copy in oct_sends:
            copy.start()

    def adapter_z():
        for copy in oct_sends:
            copy.wait_recv()
        total = pa[quarter].astype(f32)
        for index in range(3):
            total += ra[index].astype(f32)
        other_up = rb[0].astype(f32)
        for index in range(1, 4):
            other_up += rb[index].astype(f32)
        up_total = total[:ranks, :cols] + jnp.concatenate(
            [other_up[:ranks, :], other_up[ranks:, : cols - lanes]], axis=1
        )
        zb[z, :ranks, :cols] = up_total.astype(bf16)
        zb[z, ranks:, :features] = total[ranks:, :features].astype(bf16)
        for copy in z_sends:
            copy.start()

    def adapter_quad():
        for copy in z_sends:
            copy.wait_recv()
        total = zb[0].astype(f32)
        for index in range(1, z_size):
            total += zb[index].astype(f32)
        f_own[...] = total.astype(bf16)
        for copy in quad_sends + [f_copy]:
            copy.start()

    zb[z] = jnp.zeros(zb.shape[1:], bf16)
    pa[...] = jnp.zeros_like(pa)
    pb[...] = jnp.zeros_like(pb)

    def start_far(w):
        for side in range(2):

            @pl.when(has[side])
            def _():
                for copy in grad_far(w, side):
                    copy.start()

    for copy in grad_pair(0) + grad_pair(1):
        copy.start()
    start_far(0)
    adapter_parts()
    start_far(1)

    for copy in loads[5:]:
        copy.wait()
    k_pair.wait_recv()
    v_pair.wait_recv()
    dk_acc[...] = jnp.zeros_like(dk_acc)
    dv_acc[...] = jnp.zeros_like(dv_acc)
    for row in range(2):
        kt_buf[:, row * 2 * tile : (row + 1) * 2 * tile] = kb[row].T

    for side in range(2):

        @pl.when(jnp.logical_not(has[1 - side]))
        def _():
            for slot in (2 + 2 * side, 3 + 2 * side):
                qb[slot] = jnp.zeros(qb.shape[1:], bf16)
                db[slot] = jnp.zeros(db.shape[1:], bf16)
                st[slot] = jnp.zeros(st.shape[1:], f32)
            ret[side] = jnp.zeros(ret.shape[1:], bf16)

    reach_t = reach[h, 0]
    reach_h = reach[h, 1]
    reach_w = reach[h, 2]

    def locate(u):
        v = u - 2
        near = u < 2
        w = jnp.where(near, u, v // 2)
        row = lax.rem(v + 2, 2)
        slots = (jnp.where(near, 0, 2 + row), jnp.where(near, 1, 4 + row))
        return near, w, row, slots

    def back(u, side):
        _, w, row, _ = locate(u)
        where = {"tm": (left, right)[side], "space": row}
        return remote(
            rq.at[u, side],
            ret.at[1 - side, h, rows_of(w)],
            r_send.at[u, side],
            r_recv.at[2 * (1 - side) + h, w],
            where,
        )

    def back_pair(u):
        rows = rows_of(u)
        return remote(
            rq.at[u, other], ret.at[2, h, rows], r_send.at[u, other], r_recv.at[4 + h, u], partner
        )

    def arrive(slot, w):
        rows = rows_of(w)
        remote(st.at[slot, w], st.at[slot, w], s_send.at[0, 0], s_recv.at[slot, w], partner).wait_recv()
        remote(
            db.at[slot, rows], db.at[slot, rows], d_send.at[0, 0], d_recv.at[slot, w], partner
        ).wait_recv()

        @pl.when(w == 0)
        def _():
            remote(qb.at[slot], qb.at[slot], q_send.at[0], q_recv.at[slot], partner).wait_recv()

    def step(u, carry):
        near, w, row, slots = locate(u)
        rows = rows_of(w)

        @pl.when(near)
        def _():
            arrive(other, w)

        @pl.when(u == 4)
        def _():
            adapter_z()

        @pl.when(u >= 2)
        def _():
            for side in range(2):

                @pl.when(has[1 - side])
                def _():
                    arrive(slots[side], w)

        q = jnp.concatenate([qb[slot, rows, :] for slot in slots], axis=0)
        d = jnp.concatenate([db[slot, rows, :] for slot in slots], axis=0)
        lse = [st[slot, w, 0:1, :] for slot in slots]
        delta = jnp.concatenate([st[slot, w, 1:2, :] for slot in slots], axis=1)
        frame_ok = [near | ((reach_t >= 1) & (t > 0)), near | ((reach_t >= 1) & (t < t_size - 1))]
        height = [jnp.where(near, 0, row), jnp.where(near, 1, row)]
        dq = None
        for kt in range(4):
            hk, wk = kt // 2, kt % 2
            key_ok = (jnp.abs(w - wk) <= reach_w) & (valid[hk, wk, t] == 1)
            shift = jnp.concatenate(
                [
                    lse[side]
                    + jnp.where(
                        key_ok & frame_ok[side] & (jnp.abs(height[side] - hk) <= reach_h), 0.0, FAR
                    )
                    for side in range(2)
                ],
                axis=1,
            )
            k = kb[hk, wk * tile : (wk + 1) * tile, :]
            v = vb[hk, wk * tile : (wk + 1) * tile, :]
            probs = jnp.exp2(dot(k, q, NT) * (scale * LOG2E) - shift)
            dprobs = dot(v, d, NT)
            dscore = (probs * (dprobs - delta)).astype(bf16)
            span = slice(kt * tile, (kt + 1) * tile)
            dv_acc[span, :] += dot(probs.astype(bf16), d)
            dk_acc[span, :] += dot(dscore, q)
            part = dot(kt_buf[:, span], dscore)
            dq = part if dq is None else dq + part
        dq_rows = (dq * scale).T.astype(bf16)
        for side in range(2):
            rq[u, side] = dq_rows[side * tile : (side + 1) * tile, :]

        for side in range(2):

            @pl.when((u >= 2) & has[1 - side])
            def _():
                back(u, side).start()

        @pl.when(near)
        def _():
            back_pair(u).start()
            ret[2, h, rows, :] = rq[u, h]

        return carry

    lax.fori_loop(0, 6, step, 0)

    def convert(row):
        rows = pl.ds(pl.multiple_of(row * 2 * tile, 2 * tile), 2 * tile)
        dkb[row] = (dk_acc[rows, :] * scale).astype(bf16)
        dvb[row] = dv_acc[rows, :].astype(bf16)

    pair_out = [
        remote(dkb.at[other], gk.at[:, mine_lanes], out_send.at[0], out_recv.at[0], partner),
        remote(dvb.at[other], gv.at[:, mine_lanes], out_send.at[1], out_recv.at[1], partner),
    ]
    own_out = [
        pltpu.make_async_copy(dkb.at[h], gk.at[:, mine_lanes], out_sem.at[0]),
        pltpu.make_async_copy(dvb.at[h], gv.at[:, mine_lanes], out_sem.at[1]),
    ]
    convert(other)
    for copy in pair_out:
        copy.start()
    convert(h)
    for copy in own_out:
        copy.start()

    adapter_quad()

    gq_copies = [
        pltpu.make_async_copy(gq_v.at[rows_of(w)], gq.at[rows_of(w)], out_sem.at[2 + 2 * w])
        for w in range(2)
    ]
    for w in range(2):
        rows = rows_of(w)
        for side in range(2):

            @pl.when(has[1 - side])
            def _():
                for n in range(2):
                    remote(
                        ret.at[side, n, rows],
                        ret.at[side, n, rows],
                        r_send.at[0, 0],
                        r_recv.at[2 * side + n, w],
                        partner,
                    ).wait_recv()

        remote(
            ret.at[2, other, rows], ret.at[2, other, rows], r_send.at[0, 0], r_recv.at[4 + other, w], partner
        ).wait_recv()
        for n in range(2):
            total = (
                ret[0, n, rows, :].astype(f32)
                + ret[1, n, rows, :].astype(f32)
                + ret[2, n, rows, :].astype(f32)
            )
            gq_v[rows, n * hd : (n + 1) * hd] = total.astype(bf16)
        gq_copies[w].start()

    for copy in quad_sends:
        copy.wait_recv()

    for copy in sends + mx_sends + oct_sends + z_sends + quad_sends + pair_out:
        copy.wait_send()
    for w in range(2):
        for copy in grad_pair(w):
            copy.wait_send()
    for side in range(2):

        @pl.when(has[side])
        def _():
            for copy in q_sends(side):
                copy.wait_send()
            for w in range(2):
                for copy in grad_far(w, side):
                    copy.wait_send()


    def drain(u, carry):
        for side in range(2):

            @pl.when(has[1 - side])
            def _():
                back(u, side).wait_send()

        return carry

    lax.fori_loop(2, 6, drain, 0)
    for u in range(2):
        back_pair(u).wait_send()
    for copy in pair_out:
        copy.wait_recv()
    for copy in own_out + gq_copies + [f_copy]:
        copy.wait()


def finish(gq_in, gk_in, gv_in, fq_in, gq, gk, gv, ga, um, gq_v, gk_v, gv_v, fq_v, ga_v, um_v, sems):
    pairs = ((fq_in, fq_v), (gq_in, gq_v), (gk_in, gk_v), (gv_in, gv_v))
    reads = [pltpu.make_async_copy(*pair, sems.at[0, i]) for i, pair in enumerate(pairs)]
    pairs = ((ga_v, ga), (gq_v, gq), (gk_v, gk), (gv_v, gv), (um_v, um))
    writes = [pltpu.make_async_copy(*pair, sems.at[1, i]) for i, pair in enumerate(pairs)]
    for copy in reads:
        copy.start()
    for i in range(1, 4):
        reads[i].wait()
        writes[i].start()
    reads[0].wait()
    ranks = fq_v.shape[1] // 2
    for p in range(4):
        rows = slice(p * ranks, (p + 1) * ranks)
        um_v[rows, :] = fq_v[p, :ranks, : um_v.shape[1]].astype(f32)
        ga_v[rows, :] = fq_v[p, ranks:, : ga_v.shape[1]].astype(f32)
    writes[0].start()
    writes[4].start()
    for copy in writes:
        copy.wait()


def body(
    queries,
    keys,
    values,
    attention_output,
    row_logsumexp,
    output_cotangent,
    output_weight,
    adapter_down,
    adapter_up,
    head_tile_reach,
    key_tile_valid,
):
    tile = queries.shape[3]
    features = queries.shape[4]
    tokens = queries.shape[2] * tile
    heads = head_tile_reach.shape[0]
    hd = features // heads
    rank = adapter_down.shape[1]
    model = output_cotangent.shape[4]
    t_size = lax.axis_size("tm")
    g_size = lax.axis_size("tensor")
    total_tokens = t_size * lax.axis_size("space") * tokens
    cols = model // g_size
    width = max(cols, features)
    ranks = rank // 4
    lanes = -(-cols // 256) * 128
    y_size = g_size // 2
    sizes = (tile, hd, t_size, g_size, total_tokens, cols)

    def flat(array):
        return array.reshape(tokens, array.shape[-1])

    anywhere = pl.BlockSpec(memory_space=pl.ANY)
    hbm = pl.BlockSpec(memory_space=pltpu.HBM)
    dma = pltpu.SemaphoreType.DMA
    grads = jax.ShapeDtypeStruct((tokens, features), bf16)
    scratch = [
        pltpu.VMEM((6, tokens, hd), bf16),
        pltpu.VMEM((6, tokens, hd), bf16),
        pltpu.VMEM((6, 2, 8, tile), f32),
        pltpu.VMEM((2, tokens, hd), bf16),
        pltpu.VMEM((2, tokens, hd), bf16),
        pltpu.VMEM((hd, 2 * tokens), bf16),
        pltpu.VMEM((tokens, features), bf16),
        pltpu.VMEM((2, heads, tile), f32),
        pltpu.VMEM((tokens, model), bf16),
        pltpu.VMEM((features, model), bf16),
        pltpu.VMEM((rank, features), bf16),
        pltpu.VMEM((rank, model), bf16),
        pltpu.VMEM((2, tokens, hd), bf16),
        pltpu.VMEM((2, 2, 8, tile), f32),
        pltpu.VMEM((tokens, rank), bf16),
        pltpu.VMEM((2 * tokens, hd), f32),
        pltpu.VMEM((2 * tokens, hd), f32),
        pltpu.VMEM((6, 2, tile, hd), bf16),
        pltpu.VMEM((3, 2, tokens, hd), bf16),
        pltpu.VMEM((tokens, features), bf16),
        pltpu.VMEM((2, tokens, hd), bf16),
        pltpu.VMEM((2, tokens, hd), bf16),
        pltpu.VMEM((rank, tokens), bf16),
        pltpu.VMEM((max(y_size - 1, 1), rank, tokens), bf16),
        pltpu.VMEM((4, 2 * ranks, width), bf16),
        pltpu.VMEM((4, 2 * ranks, lanes), bf16),
        pltpu.VMEM((3, 2 * ranks, width), bf16),
        pltpu.VMEM((4, 2 * ranks, lanes), bf16),
        pltpu.VMEM((t_size // 2, 2 * ranks, width), bf16),
        pltpu.VMEM((2 * ranks, width), bf16),
        pltpu.SMEM(head_tile_reach.shape, jnp.int32),
        pltpu.SMEM(key_tile_valid.shape[1:] + key_tile_valid.shape[:1], jnp.int32),
        dma((12,)),
        dma((5,)),
        dma((6,)),
        dma((2, 5)),
        dma((6, 2)),
        dma((2, 5)),
        dma((6, 2)),
        dma((2,)),
        dma((2,)),
        dma((6, 2)),
        dma((6, 2)),
        dma((max(y_size - 1, 1),)),
        dma((max(y_size - 1, 1),)),
        dma((7,)),
        dma((7,)),
        dma((t_size // 2 - 1,)),
        dma((t_size // 2 - 1,)),
        dma((3,)),
        dma((3,)),
        dma((2,)),
        dma((2,)),
        dma((5,)),
    ]
    results = pl.pallas_call(
        functools.partial(kernel, sizes),
        out_shape=(
            grads,
            grads,
            grads,
            jax.ShapeDtypeStruct((4, 2 * ranks, width), bf16),
        ),
        in_specs=[hbm] * 11,
        out_specs=(anywhere,) * 4,
        scratch_shapes=scratch,
        compiler_params=pltpu.CompilerParams(
            collective_id=0, has_side_effects=True, vmem_limit_bytes=62 * 1024 * 1024
        ),
    )(
        flat(queries),
        flat(keys),
        flat(values),
        flat(attention_output),
        row_logsumexp.reshape(row_logsumexp.shape[2:]),
        flat(output_cotangent),
        output_weight,
        adapter_down.T,
        adapter_up,
        head_tile_reach,
        jnp.transpose(key_tile_valid, (1, 2, 0)),
    )
    totals = (jax.ShapeDtypeStruct((rank, features), f32), jax.ShapeDtypeStruct((rank, cols), f32))
    grad_q, grad_k, grad_v, grad_a, up_map_gradient = pl.pallas_call(
        finish,
        out_shape=(grads, grads, grads, *totals),
        in_specs=[anywhere] * 4,
        out_specs=(anywhere,) * 5,
        scratch_shapes=[pltpu.VMEM(array.shape, array.dtype) for array in (*results, *totals)]
        + [dma((2, 5))],
        compiler_params=pltpu.CompilerParams(vmem_limit_bytes=62 * 1024 * 1024),
    )(*results)
    return (
        grad_q.reshape(queries.shape),
        grad_k.reshape(queries.shape),
        grad_v.reshape(queries.shape),
        grad_a.T,
        up_map_gradient,
    )


def solution(mesh):
    placed = (
        P("tm", "space", None, None, "tensor"),
        P("tm", "space", None, None, "tensor"),
        P("tm", "space", None, None, "tensor"),
        P("tm", "space", None, None, "tensor"),
        P("tm", "space", None, "tensor", None),
        P("tm", "space", None, None, None),
        P("tensor", None),
        P("tensor", None),
        P(),
        P("tensor", None),
        P(),
    )
    return jax.shard_map(
        body,
        mesh=mesh,
        in_specs=placed,
        out_specs=(
            P("tm", "space", None, None, "tensor"),
            P("tm", "space", None, None, "tensor"),
            P("tm", "space", None, None, "tensor"),
            P("tensor", None),
            P(None, "tensor"),
        ),
        check_vma=False,
    )
```
